512 devices in a mesh: blk: 128 (over z, y, core), view: 4 (over x).
Axes of the slice: x: 4, y: 8, z: 8, core: 2. Of those that a mesh axis runs over, the one named last changes fastest.
Arguments:
- estimate: float32 [4096, 64, 128], P('blk'), may hold values from 0.5 to 2
- view_data: float32 [4, 4096, 64, 128], P('view', 'blk'), may hold values from 0.25 to 4
- slot_block: int32 [4, 128], P('view', 'blk'), may hold values from 0 to 127, each once within a row
- offsets: int32 [4, 128], P('view', 'blk'), may hold values from -8 to 8
- taps: float32 [4, 3, 31], P('view'), may hold values from 0.02 to 1
Outputs:
- deconvolved: float32 [4096, 64, 128], P('blk')
The draws below stay inside these ranges and needn't reach their ends.
Inputs may be any that keep to these rules, and one draw needn't show every extreme that they name: `slot_block`: each view's row names every block once.
All inputs are finite; a program needn't handle non-finite values.
Results may differ from the reference program's by a relative error of at most 0.0001.
Values sent between devices are 32-bit elements; how exact they have to be, the bound alone decides.
A program may use at most 64 MiB of HBM per device.

```python
import math
import jax
import jax.numpy as jnp
from jax import lax

BX = 32
Y = 64
Z = 128
TAPS = 31
SHIFT = 8
ITERS = 2
HALF = 15
RIM = 23
VIEWS = 4
X = 4096
N_BLK = 128


def touch_ends(array, key, least, largest):
    place = [jax.random.randint(jax.random.fold_in(key, axis), (), 0, length) for axis, length in enumerate(array.shape)]
    main_axis = array.shape.index(max(array.shape))
    beside = place[:main_axis] + [(place[main_axis] + 1) % array.shape[main_axis]] + place[main_axis + 1:]
    return array.at[tuple(place)].set(least).at[tuple(beside)].set(largest)


def level_of(rng, extent, cuts, smallest, high):
    gain = 1.0
    for dim, blocks in cuts:
        draws = jax.random.uniform(jax.random.fold_in(jax.random.fold_in(rng, 6), dim), (blocks,), jnp.float32, smallest / len(cuts), high / len(cuts))
        gain = gain * jnp.repeat(jnp.exp(draws), extent[dim] // blocks).reshape((-1,) + (1,) * (len(extent) - 1 - dim))
    return gain


def setup_inputs(seed: int = 0) -> dict:
    keys = jax.random.split(jax.random.key(seed), 6)
    estimate = jnp.clip(jnp.exp(math.log(2.0) - 1.3862944 * jax.random.uniform(keys[0], (X, Y, Z), jnp.float32) ** level_of(keys[0], (X, Y, Z), ((0, 128),), -0.2, 0.2)), 0.5, 2.0)
    view_data = jnp.clip(jnp.exp(math.log(4.0) - 2.7725887 * jax.random.uniform(keys[1], (VIEWS, X, Y, Z), jnp.float32) ** level_of(keys[1], (VIEWS, X, Y, Z), ((0, 4), (1, 128)), -0.2, 0.2)), 0.25, 4.0)
    slot_block = jax.vmap(lambda own: jax.random.permutation(own, N_BLK))(jax.random.split(keys[2], VIEWS)).reshape((VIEWS, N_BLK)).astype(jnp.int32)
    offsets = touch_ends(jax.random.randint(keys[3], (VIEWS, N_BLK), 0 - SHIFT, SHIFT + 1), jax.random.fold_in(keys[3], 1), 0 - SHIFT, SHIFT).astype(jnp.int32)
    taps = jnp.clip(jnp.exp(math.log(1.0) - 3.912023 * jax.random.uniform(keys[4], (VIEWS, 3, TAPS), jnp.float32) ** level_of(keys[4], (VIEWS, 3, TAPS), ((0, 4),), -0.2, 0.2)), 0.02, 1.0)
    return dict(estimate=estimate, view_data=view_data, slot_block=slot_block, offsets=offsets, taps=taps)


HIGHEST = lax.Precision.HIGHEST


def banded(weights, offsets_table):
    hits = offsets_table[..., None] == jnp.arange(TAPS, dtype=jnp.int32)
    return jnp.sum(jnp.where(hits, weights, jnp.float32(0.0)), axis=-1)


def toeplitz(length):
    index = jnp.arange(length, dtype=jnp.int32)
    return index[None, :] - index[:, None] + HALF


def reference(estimate, view_data, slot_block, offsets, taps):
    current = estimate
    window_rows = BX + 2 * RIM
    row_index = (jnp.arange(N_BLK, dtype=jnp.int32) * BX)[:, None] + jnp.arange(window_rows, dtype=jnp.int32)[None, :]
    x_index = jnp.arange(BX, dtype=jnp.int32)
    w_index = jnp.arange(window_rows, dtype=jnp.int32)
    for iteration in range(ITERS):
        padded = jnp.pad(current, ((RIM, RIM), (0, 0), (0, 0)))
        windows = padded[row_index]
        summed = jnp.zeros_like(current)
        for view_index in range(VIEWS):
            kernel = taps[view_index] / jnp.sum(taps[view_index], axis=-1, keepdims=True)
            mat_y = banded(kernel[1], toeplitz(Y))
            mat_z = banded(kernel[2], toeplitz(Z))
            shift_table = w_index[None, None, :] - RIM - offsets[view_index][:, None, None] - x_index[None, :, None] + HALF
            mat_x = banded(kernel[0], shift_table.astype(jnp.int32))
            measured = jnp.zeros((N_BLK, BX, Y, Z), jnp.float32).at[slot_block[view_index]].set(
                view_data[view_index].reshape(N_BLK, BX, Y, Z))
            blur_x = jnp.einsum('jxw,jwyz->jxyz', mat_x, windows, precision=HIGHEST)
            blur_y = jnp.einsum('jxqz,pq->jxpz', blur_x, mat_y, precision=HIGHEST)
            blur_z = jnp.einsum('jxyq,pq->jxyp', blur_y, mat_z, precision=HIGHEST)
            ratios = measured / blur_z
            back_z = jnp.einsum('jxyp,pq->jxyq', ratios, mat_z, precision=HIGHEST)
            back_y = jnp.einsum('jxpz,pq->jxqz', back_z, mat_y, precision=HIGHEST)
            back_w = jnp.einsum('jxw,jxyz->jwyz', mat_x, back_y, precision=HIGHEST)
            spread_out = jnp.zeros((X + 2 * RIM, Y, Z), jnp.float32).at[row_index].add(back_w)
            summed = summed + spread_out[RIM:RIM + X]
        current = current * (summed / VIEWS)
    return current
```

```python
import jax
import jax.numpy as jnp
from jax import lax
from jax.sharding import PartitionSpec as P

ITERS = 2
HALF = 15
RIM = 23


HIGHEST = lax.Precision.HIGHEST


def extended_2(value, sides, width):
    for axis, dim in sides:
        size, length = (lax.axis_size(axis), value.shape[dim])
        up = [(i, (i + 1) % size) for i in range(size - 1)]
        down = [(j, i) for i, j in up]
        last = lax.slice_in_dim(value, length - width, length, axis=dim)
        leading = lax.slice_in_dim(value, 0, width, axis=dim)
        before = lax.ppermute(last, axis, up)
        after = lax.ppermute(leading, axis, down)
        value = jnp.concatenate([before, value, after], axis=dim)
    return value


def banded(weights, offsets_table):
    hits = offsets_table[..., None] == jnp.arange(weights.shape[0], dtype=jnp.int32)
    return jnp.sum(jnp.where(hits, weights, jnp.float32(0.0)), axis=-1)


def toeplitz(length):
    index = jnp.arange(length, dtype=jnp.int32)
    return index[None, :] - index[:, None] + HALF


def relay_blocks(block, source_of, blocks_count):
    pieces = block.reshape(blocks_count, -1)
    exchanged = lax.all_to_all(pieces, "blk", split_axis=0, concat_axis=0, tiled=True)
    chosen = jnp.take(exchanged, source_of, axis=0)
    returned = lax.all_to_all(chosen, "blk", split_axis=0, concat_axis=0, tiled=True)
    return returned.reshape(block.shape)


def blur_and_back(blur_x, measured, mat_y, mat_z):
    blur_y = jnp.einsum("xqz,pq->xpz", blur_x, mat_y, precision=HIGHEST)
    blur_z = jnp.einsum("xyq,pq->xyp", blur_y, mat_z, precision=HIGHEST)
    ratios = measured / blur_z
    back_z = jnp.einsum("xyp,pq->xyq", ratios, mat_z, precision=HIGHEST)
    return jnp.einsum("xpz,pq->xqz", back_z, mat_y, precision=HIGHEST)


def per_device(estimate, view_data, slot_block, offsets, taps):
    blocks_count = lax.axis_size("blk")
    view_count = lax.axis_size("view")
    block_rows = estimate.shape[0]
    window_rows = block_rows + 2 * RIM
    kernel = taps[0] / jnp.sum(taps[0], axis=-1, keepdims=True)
    mat_y = banded(kernel[1], toeplitz(estimate.shape[1]))
    mat_z = banded(kernel[2], toeplitz(estimate.shape[2]))
    x_index = jnp.arange(block_rows, dtype=jnp.int32)
    w_index = jnp.arange(window_rows, dtype=jnp.int32)
    shift_table = w_index[None, :] - RIM - offsets[0, 0] - x_index[:, None] + HALF
    mat_x = banded(kernel[0], shift_table)
    listing = lax.all_gather(slot_block, "blk", axis=1, tiled=True)[0]
    slot_ids = jnp.arange(blocks_count, dtype=jnp.int32)
    holder_of = jnp.sum(
        jnp.where(listing[None, :] == slot_ids[:, None], slot_ids[None, :], 0), axis=1
    )
    measured = relay_blocks(view_data[0], holder_of, blocks_count)
    current = estimate
    for iteration in range(ITERS):
        extended = extended_2(current, (("blk", 0),), RIM)
        blur_x = jnp.einsum("xw,wyz->xyz", mat_x, extended, precision=HIGHEST)
        back_y = blur_and_back(blur_x, measured, mat_y, mat_z)
        back_w = jnp.einsum("xw,xyz->wyz", mat_x, back_y, precision=HIGHEST)
        rim_rows = jnp.concatenate([back_w[:RIM], back_w[RIM + block_rows :]], axis=0)
        neighbour_rims = extended_2(rim_rows, (("blk", 0),), RIM)
        own_rows = back_w[RIM : RIM + block_rows]
        own_rows = own_rows + jnp.pad(neighbour_rims[:RIM], ((0, block_rows - RIM), (0, 0), (0, 0)))
        own_rows = own_rows + jnp.pad(
            neighbour_rims[3 * RIM :], ((block_rows - RIM, 0), (0, 0), (0, 0))
        )
        summed = lax.psum(own_rows, "view")
        current = current * (summed / view_count)
    return current


def solution(mesh):
    return jax.shard_map(
        per_device,
        mesh=mesh,
        in_specs=(
            P("blk", None, None),
            P("view", "blk", None, None),
            P("view", "blk"),
            P("view", "blk"),
            P("view", None, None),
        ),
        out_specs=P("blk", None, None),
        check_vma=False,
    )
```

```python
import functools

import jax
import jax.numpy as jnp
from jax import lax
from jax.experimental import pallas as pl
from jax.experimental.pallas import tpu as pltpu
from jax.sharding import PartitionSpec as P

ITERS = 2
HALF = 15
VIEWS = 4
SUB = 16
EDGE = 24
WIN = SUB + 2 * EDGE
CHUNKS = 4
MESH = pl.DeviceIdType.MESH
F32 = jnp.float32
BF16 = jnp.bfloat16


def split(value):
    high = value.astype(BF16)
    low = (value - high.astype(F32)).astype(BF16)
    return high, low


def dot(a, b):
    return jnp.dot(a, b, preferred_element_type=F32)


def left_pack(weights):
    high, low = split(weights)
    return jnp.concatenate([high, high, low], axis=1)


def right_pack(weights):
    high, low = split(weights)
    top = jnp.concatenate([high, low], axis=1)
    bottom = jnp.concatenate([high, jnp.zeros_like(high)], axis=1)
    return jnp.concatenate([top, bottom], axis=0)


def from_left(packed, value):
    high, low = split(value)
    return dot(packed, jnp.concatenate([high, low, high], axis=0))


def from_right(value, packed):
    high, low = split(value)
    both = dot(jnp.concatenate([high, low], axis=1), packed)
    half = both.shape[1] // 2
    return both[:, :half] + both[:, half:]


def to_lanes(rows, depth):
    return jnp.concatenate([rows[i : i + depth] for i in range(0, rows.shape[0], depth)], axis=1)


def to_rows(lanes, width):
    return jnp.concatenate([lanes[:, i : i + width] for i in range(0, lanes.shape[1], width)], axis=0)


def kernel(
    n_blk, row_size, y_cells, z_cells,
    slot_ref, mx_ref, w_ref, est_ref, view_ref,
    out_ref,
    id_own, id_row, id_all, inv_v, inv_s,
    exch, chosen, meas,
    mx_all, w_all, mxc, mxtc, wyc, wytc, wzc, wztc,
    est_half, est_flat, win, yz, stage, blurred, back_full, back_recv, corr,
    from_m1, from_p1, from_m2, from_p2, out_flat, out_half,
    id1_send, id1_recv, id2_send, id2_recv, inv_sem,
    p1_send, p1_recv, p2_send, p2_recv,
    mx_send, mx_recv, w_send, w_recv, est_send, est_recv,
    halo_send, halo_recv, x_send, x_recv, b_send, b_recv, c_send, c_recv, o_send, o_recv,
    in_row, in_plane,
):
    y_half = y_cells // 2
    y_chunk = y_half // CHUNKS
    lanes = y_chunk * z_cells
    pieces, piece_rows = view_ref.shape[0], view_ref.shape[1]
    half_pieces = pieces // 2
    n_rows = n_blk // row_size
    chips = 2 * n_blk

    x = lax.axis_index("view")
    b = lax.axis_index("blk")
    a = lax.rem(b, 2)
    c = b // 2
    other = 1 - a

    def snake(q, line):
        return q + lax.rem(line, 2) * (3 - 2 * q)

    q = snake(x, c)
    n = 4 * c + q
    partner = (x, 2 * c + other)
    row, place = b // row_size, lax.rem(b, row_size)

    def along(step):
        m = lax.rem(n + step + chips, chips)
        line = m // 4
        return (snake(lax.rem(m, 4), line), 2 * line + a)

    def device(view_blk):
        return {"view": view_blk[0], "blk": view_blk[1]}

    def remote(src, dst, send, recv, where):
        return pltpu.make_async_remote_copy(
            src_ref=src, dst_ref=dst, send_sem=send, recv_sem=recv,
            device_id=device(where), device_id_type=MESH,
        )

    def await_bytes(ref, sem):
        pltpu.make_async_copy(ref, ref, sem).wait()

    line_mates = []
    for step in range(1, 4):
        line_mates.append((lax.rem(x + step, 4), b))
    for step in range(4):
        line_mates.append((lax.rem(x + step, 4), 2 * c + other))
    chain = {step: along(step) for step in (-2, -1, 1, 2)}

    barrier = pltpu.get_barrier_semaphore()

    def greet_row(i, carry):
        mate = row * row_size + lax.rem(place + i, row_size)
        pl.semaphore_signal(barrier, inc=1, device_id=device((x, mate)), device_id_type=MESH)
        return carry

    def greet_column(i, carry):
        mate = lax.rem(row + i, n_rows) * row_size + place
        pl.semaphore_signal(barrier, inc=1, device_id=device((x, mate)), device_id_type=MESH)
        return carry

    lax.fori_loop(1, row_size, greet_row, 0)
    lax.fori_loop(1, n_rows, greet_column, 0)
    for mate in line_mates + list(chain.values()):
        pl.semaphore_signal(barrier, inc=1, device_id=device(mate), device_id_type=MESH)
    pl.semaphore_wait(barrier, row_size - 1 + n_rows - 1 + len(line_mates) + len(chain))

    def tell_column(i, carry):
        mate = lax.rem(row + i, n_rows) * row_size + place
        pl.semaphore_signal(in_row, inc=1, device_id=device((x, mate)), device_id_type=MESH)
        return carry

    lax.fori_loop(1, n_rows, tell_column, 0)

    id_own[...] = jnp.full(id_own.shape, slot_ref[0, 0], jnp.int32)

    def send_id(i, carry):
        mate = row * row_size + lax.rem(place + i, row_size)
        remote(id_own, id_row.at[place], id1_send, id1_recv, (x, mate)).start()
        return carry

    lax.fori_loop(1, row_size, send_id, 0)
    id_row[place] = id_own[...]

    par = q // 2
    rows_here = pl.ds(pl.multiple_of(lax.rem(q, 2) * SUB, SUB), SUB)

    def est_part(core):
        return est_ref.at[rows_here, pl.ds(pl.multiple_of(core * y_half, y_half), y_half), :]

    @pl.when(a == par)
    def _():
        remote(est_part(other), est_half, est_send, est_recv, partner).start()
        pltpu.make_async_copy(est_part(a), est_half, est_recv).start()

    for i, mate in enumerate(line_mates):
        remote(mx_ref, mx_all.at[a, x], mx_send.at[i], mx_recv.at[i], mate).start()
    mx_all[a, x] = mx_ref[...]
    for i in range(3):
        remote(w_ref, w_all.at[x], w_send.at[i], w_recv.at[i], line_mates[i]).start()
    w_all[x] = w_ref[...]

    pl.semaphore_wait(in_row, n_rows - 1)
    for step in range(1, 4):
        pl.semaphore_signal(
            in_plane, inc=1, device_id=device((lax.rem(x + step, 4), b)), device_id_type=MESH
        )

    def scatter(i, carry):
        to = lax.rem(b + i, n_blk)
        remote(view_ref.at[to], exch.at[b], p1_send, p1_recv, (x, to)).start()
        return carry

    lax.fori_loop(1, n_blk, scatter, 0)
    pltpu.make_async_copy(view_ref.at[b], exch.at[b], p1_recv).start()

    halo_plan = (
        (1, slice(EDGE, EDGE + SUB), slice(EDGE - SUB, EDGE)),
        (-1, slice(EDGE, EDGE + SUB), slice(EDGE + SUB, EDGE + 2 * SUB)),
        (2, slice(EDGE + SUB - 8, EDGE + SUB), slice(0, 8)),
        (-2, slice(EDGE, EDGE + 8), slice(WIN - 8, WIN)),
    )

    def halo_copies(it, ch):
        cols = slice(ch * lanes, (ch + 1) * lanes)
        return [
            remote(win.at[it, src, cols], win.at[it, dst, cols],
                   halo_send.at[it, ch, i], halo_recv.at[it, ch, i], chain[step])
            for i, (step, src, dst) in enumerate(halo_plan)
        ]

    corr_plan = (
        (1, slice(EDGE + SUB, EDGE + 2 * SUB), from_m1),
        (-1, slice(EDGE - SUB, EDGE), from_p1),
        (2, slice(WIN - 8, WIN), from_m2),
        (-2, slice(0, 8), from_p2),
    )

    def corr_copies(it, ch):
        cols = slice(ch * lanes, (ch + 1) * lanes)
        return [
            remote(corr.at[it, src, cols], dst.at[it, :, cols],
                   c_send.at[it, ch, i], c_recv.at[it, ch, i], chain[step])
            for i, (step, src, dst) in enumerate(corr_plan)
        ]

    await_bytes(est_half, est_recv)
    est_flat[...] = est_half[...].reshape(est_flat.shape)
    for ch in range(CHUNKS):
        for y in range(y_chunk):
            at = ch * y_chunk + y
            win[0, EDGE : EDGE + SUB, at * z_cells : (at + 1) * z_cells] = est_flat[
                pl.ds(at, SUB, stride=y_half), :
            ]
        for copy in halo_copies(0, ch):
            copy.start()

    await_bytes(id_row.at[: row_size - 1], id1_recv)
    padded = id_all.shape[1]
    sub = lax.broadcasted_iota(jnp.int32, (padded, 128), 0)
    ids = jnp.zeros((padded, 128), jnp.int32)
    for s in range(row_size):
        ids = jnp.where(sub == s, jnp.broadcast_to(id_row[s, 0:1, :], (padded, 128)), ids)
    id_all[row] = ids

    def send_row(i, carry):
        mate = lax.rem(row + i, n_rows) * row_size + place
        remote(id_all.at[row], id_all.at[row], id2_send, id2_recv, (x, mate)).start()
        return carry

    lax.fori_loop(1, n_rows, send_row, 0)

    for i, mate in enumerate(line_mates):
        remote(mx_ref, mx_all.at[a, x], mx_send.at[i], mx_recv.at[i], mate).wait_recv()
    mine, yours = 2 * a, 2 * other
    mat = jnp.concatenate(
        [mx_all[par, v] for v in (mine, mine + 1, yours, yours + 1)], axis=0
    )
    reach = lax.broadcasted_iota(jnp.int32, mat.shape, 1) + (n * SUB - EDGE)
    mat = jnp.where((reach >= 0) & (reach < chips * SUB), mat, F32(0.0))
    mxc[...] = left_pack(mat[:, :WIN])
    mxtc[...] = left_pack(jnp.transpose(mat)[:WIN, :])

    def blur_x(it, ch):
        for copy in halo_copies(it, ch):
            copy.wait_recv()
        out = from_left(mxc[...], win[it, :, ch * lanes : (ch + 1) * lanes])
        for y in range(y_chunk):
            part = out[:, y * z_cells : (y + 1) * z_cells]
            stage[it, ch, pl.ds(y, 2 * SUB, stride=y_chunk), :] = part[2 * SUB :]
        x_copy(it, ch).start()
        for y in range(y_chunk):
            part = out[:, y * z_cells : (y + 1) * z_cells]
            yz[it, a, ch, pl.ds(y, 2 * SUB, stride=y_chunk), :] = part[: 2 * SUB]

    def x_copy(it, ch):
        return remote(
            stage.at[it, ch], yz.at[it, a, ch], x_send.at[it, ch], x_recv.at[it, ch], partner
        )

    for ch in range(CHUNKS):
        blur_x(0, ch)

    for i in range(3):
        remote(w_ref, w_all.at[x], w_send.at[i], w_recv.at[i], line_mates[i]).wait_recv()
    for v in range(2):
        w = w_all[mine + v]
        wyc[v] = left_pack(w[:y_cells, :y_cells])
        wytc[v] = left_pack(w[:y_cells, y_cells : 2 * y_cells])
        wztc[v] = right_pack(w[y_cells : y_cells + z_cells])
        wzc[v] = right_pack(w[y_cells + z_cells :])

    await_bytes(id_all.at[: n_rows - 1], id2_recv)
    slot = lax.broadcasted_iota(jnp.int32, id_all.shape, 0) * row_size + lax.broadcasted_iota(
        jnp.int32, id_all.shape, 1
    )
    real = lax.broadcasted_iota(jnp.int32, id_all.shape, 1) < row_size
    hit = (id_all[...] == lax.broadcasted_iota(jnp.int32, id_all.shape, 2)) & real
    found = jnp.max(jnp.where(hit, slot, 0), axis=0)
    found = jnp.max(found, axis=0, keepdims=True)
    inv_v[...] = jnp.broadcast_to(found, inv_v.shape)
    to_scalars = pltpu.make_async_copy(inv_v, inv_s, inv_sem)
    to_scalars.start()
    to_scalars.wait()
    await_bytes(exch, p1_recv)
    pl.semaphore_wait(in_plane, 3)

    half = b // half_pieces
    meas_at = lax.rem(x, 2) * half_pieces + lax.rem(b, half_pieces)
    dst_piece = meas.at[pl.ds(pl.multiple_of(meas_at * piece_rows, 8), piece_rows), :]

    def forward(i, carry):
        j = lax.rem(b + i, n_blk)
        chosen[j] = exch[inv_s[0, j]]
        line = j // 2
        to_x = snake(2 * lax.rem(j, 2) + half, line)
        to_b = 2 * line + x // 2
        same = (to_x == x) & (to_b == b)

        @pl.when(same)
        def _():
            pltpu.make_async_copy(chosen.at[j], dst_piece, p2_recv).start()

        @pl.when(jnp.logical_not(same))
        def _():
            remote(chosen.at[j], dst_piece, p2_send, p2_recv, (to_x, to_b)).start()

        return carry

    lax.fori_loop(0, n_blk, forward, 0)

    group = 4

    def blur_yz(it, g):
        v = g // (SUB // group)
        rows = pl.ds(pl.multiple_of(g * (group * y_chunk), 8), group * y_chunk)
        blocks = [yz[it, h, ch, rows, :] for h in range(2) for ch in range(CHUNKS)]
        value = jnp.concatenate(
            [block[r * y_chunk : (r + 1) * y_chunk] for r in range(group) for block in blocks], axis=0
        )
        value = from_right(value, wzc[v])
        return from_left(wyc[v], to_lanes(value, y_cells))

    def back_yz(it, g, blur):
        v = g // (SUB // group)
        rows = pl.ds(pl.multiple_of(g * (group * y_cells), 8), group * y_cells)
        ratios = to_lanes(meas[rows, :], y_cells) / blur
        value = to_rows(from_left(wytc[v], ratios), z_cells)
        value = from_right(value, wztc[v])
        rows = pl.ds(pl.multiple_of(g * (group * y_half), 8), group * y_half)
        for h in range(2):
            back_full[it, h, rows, :] = jnp.concatenate(
                [value[r : r + y_half] for r in range(h * y_half, value.shape[0], y_cells)], axis=0
            )

    def back_copy(it, v):
        rows = slice(v * SUB * y_half, (v + 1) * SUB * y_half)
        return remote(
            back_full.at[it, other, rows, :], back_recv.at[it, rows, :],
            b_send.at[it, v], b_recv.at[it, v], partner,
        )

    def back_x(it, ch):
        parts = []
        for y in range(y_chunk):
            rows = pl.ds(ch * y_chunk + y, 2 * SUB, stride=y_half)
            parts.append(
                jnp.concatenate([back_full[it, a, rows, :], back_recv[it, rows, :]], axis=0)
            )
        corr[it, :, ch * lanes : (ch + 1) * lanes] = from_left(mxtc[...], jnp.concatenate(parts, axis=1))
        for copy in corr_copies(it, ch):
            copy.start()

    def updated(it, ch):
        for copy in corr_copies(it, ch):
            copy.wait_recv()
        cols = slice(ch * lanes, (ch + 1) * lanes)
        total = corr[it, EDGE : EDGE + SUB, cols] + from_m1[it, :, cols] + from_p1[it, :, cols]
        total = total + jnp.concatenate([from_m2[it, :, cols], from_p2[it, :, cols]], axis=0)
        return win[it, EDGE : EDGE + SUB, cols] * (total / VIEWS)

    def out_cols(ch, core):
        return pl.ds(pl.multiple_of(core * y_half + ch * y_chunk, 8), y_chunk)

    def out_copies(ch):
        src = out_half.at[:, ch * y_chunk : (ch + 1) * y_chunk, :]
        dst = out_ref.at[rows_here, out_cols(ch, a), :]
        own = pltpu.make_async_copy(src, dst, o_recv)
        mates = [
            remote(src, dst, o_send.at[ch, i], o_recv, (lax.rem(x + i, 4), 2 * c + par))
            for i in range(4)
        ]
        return own, mates

    for it in range(ITERS):
        for ch in range(CHUNKS):
            x_copy(it, ch).wait_recv()
        if it == 0:
            def first(g, carry):
                blurred[g] = blur_yz(0, g)
                return carry

            lax.fori_loop(0, 2 * SUB // group, first, 0)
            await_bytes(meas, p2_recv)
        per_view = SUB // group
        for v in range(2):
            def both(g, carry):
                back_yz(it, g, blurred[g] if it == 0 else blur_yz(it, g))
                return carry

            lax.fori_loop(v * per_view, (v + 1) * per_view, both, 0)
            back_copy(it, v).start()
        for v in range(2):
            back_copy(it, v).wait_recv()
        for ch in range(CHUNKS):
            back_x(it, ch)
        for ch in range(CHUNKS):
            new = updated(it, ch)
            if it + 1 < ITERS:
                win[it + 1, EDGE : EDGE + SUB, ch * lanes : (ch + 1) * lanes] = new
                for copy in halo_copies(it + 1, ch):
                    copy.start()
            else:
                for y in range(y_chunk):
                    out_flat[ch, pl.ds(y, SUB, stride=y_chunk), :] = new[
                        :, y * z_cells : (y + 1) * z_cells
                    ]
                out_half[:, ch * y_chunk : (ch + 1) * y_chunk, :] = out_flat[ch].reshape(
                    SUB, y_chunk, z_cells
                )
                own, mates = out_copies(ch)
                for mate in mates[1:]:
                    mate.start()

                @pl.when(a == par)
                def _():
                    own.start()

                @pl.when(a != par)
                def _():
                    mates[0].start()
        if it + 1 < ITERS:
            for ch in range(CHUNKS):
                blur_x(it + 1, ch)

    await_bytes(id_row.at[: row_size - 1], id1_send)
    await_bytes(id_all.at[: n_rows - 1], id2_send)
    await_bytes(exch.at[: n_blk - 1], p1_send)
    await_bytes(chosen.at[: n_blk - 1], p2_send)

    @pl.when(jnp.logical_not((a == x // 2) & (lax.rem(q, 2) == half)))
    def _():
        await_bytes(chosen.at[0], p2_send)

    @pl.when(a == par)
    def _():
        remote(est_part(other), est_half, est_send, est_recv, partner).wait_send()

    for i, mate in enumerate(line_mates):
        remote(mx_ref, mx_all.at[a, x], mx_send.at[i], mx_recv.at[i], mate).wait_send()
    for i in range(3):
        remote(w_ref, w_all.at[x], w_send.at[i], w_recv.at[i], line_mates[i]).wait_send()
    for it in range(ITERS):
        for ch in range(CHUNKS):
            for copy in halo_copies(it, ch) + corr_copies(it, ch) + [x_copy(it, ch)]:
                copy.wait_send()
        for v in range(2):
            back_copy(it, v).wait_send()
    for ch in range(CHUNKS):
        own, mates = out_copies(ch)
        for mate in mates[1:]:
            mate.wait_send()

        @pl.when(a != par)
        def _():
            mates[0].wait_send()

    await_bytes(out_ref, o_recv)


def banded(weights, offsets_table):
    hits = offsets_table[..., None] == jnp.arange(weights.shape[0], dtype=jnp.int32)
    return jnp.sum(jnp.where(hits, weights, F32(0.0)), axis=-1)


def shifts(rows, columns):
    return jnp.arange(columns, dtype=jnp.int32)[None, :] - jnp.arange(rows, dtype=jnp.int32)[:, None]


def per_device(estimate, view_data, slot_block, offsets, taps):
    n_blk = lax.axis_size("blk")
    block_rows, y_cells, z_cells = estimate.shape
    row_size = 16 if n_blk % 16 == 0 else n_blk // 2
    n_rows = n_blk // row_size
    padded = max(row_size, 8)
    piece_rows = block_rows * y_cells // n_blk
    weights = taps[0] / jnp.sum(taps[0], axis=-1, keepdims=True)
    mat_x = banded(weights[0], shifts(SUB, 128) - (EDGE - HALF) - offsets[0, 0])
    mat_y = banded(weights[1], shifts(y_cells, y_cells) + HALF)
    mat_z = banded(weights[2], shifts(z_cells, z_cells) + HALF)
    tables = jnp.concatenate(
        [jnp.concatenate([mat_y, mat_y.T], axis=1), mat_z, mat_z.T], axis=0
    )
    pieces = view_data.reshape(n_blk, piece_rows, z_cells)
    y_half = y_cells // 2
    y_chunk = y_half // CHUNKS
    width = y_half * z_cells
    vmem = pltpu.VMEM
    dma = pltpu.SemaphoreType.DMA
    regular = pltpu.SemaphoreType.REGULAR
    return pl.pallas_call(
        functools.partial(kernel, n_blk, row_size, y_cells, z_cells),
        out_shape=jax.ShapeDtypeStruct(estimate.shape, F32),
        in_specs=[
            pl.BlockSpec(memory_space=pltpu.SMEM),
            pl.BlockSpec(memory_space=pltpu.VMEM),
            pl.BlockSpec(memory_space=pltpu.VMEM),
            pl.BlockSpec(memory_space=pl.ANY),
            pl.BlockSpec(memory_space=pl.ANY),
        ],
        out_specs=pl.BlockSpec(memory_space=pl.ANY),
        scratch_shapes=[
            vmem((8, 128), jnp.int32),
            vmem((row_size, 8, 128), jnp.int32),
            vmem((n_rows, padded, 128), jnp.int32),
            vmem((8, 128), jnp.int32),
            pltpu.SMEM((8, 128), jnp.int32),
            vmem((n_blk, piece_rows, z_cells), F32),
            vmem((n_blk, piece_rows, z_cells), F32),
            vmem((2 * SUB * y_cells, z_cells), F32),
            vmem((2, VIEWS, SUB, 128), F32),
            vmem((VIEWS,) + tables.shape, F32),
            vmem((4 * SUB, 3 * WIN), BF16),
            vmem((WIN, 3 * 4 * SUB), BF16),
            vmem((2, y_cells, 3 * y_cells), BF16),
            vmem((2, y_cells, 3 * y_cells), BF16),
            vmem((2, 2 * z_cells, 2 * z_cells), BF16),
            vmem((2, 2 * z_cells, 2 * z_cells), BF16),
            vmem((SUB, y_half, z_cells), F32),
            vmem((SUB * y_half, z_cells), F32),
            vmem((ITERS, WIN, width), F32),
            vmem((ITERS, 2, CHUNKS, 2 * SUB * y_chunk, z_cells), F32),
            vmem((ITERS, CHUNKS, 2 * SUB * y_chunk, z_cells), F32),
            vmem((2 * SUB // 4, y_cells, 4 * z_cells), F32),
            vmem((ITERS, 2, 2 * SUB * y_half, z_cells), F32),
            vmem((ITERS, 2 * SUB * y_half, z_cells), F32),
            vmem((ITERS, WIN, width), F32),
            vmem((ITERS, SUB, width), F32),
            vmem((ITERS, SUB, width), F32),
            vmem((ITERS, 8, width), F32),
            vmem((ITERS, 8, width), F32),
            vmem((CHUNKS, SUB * y_chunk, z_cells), F32),
            vmem((SUB, y_half, z_cells), F32),
            dma, dma, dma, dma, dma,
            dma, dma, dma, dma,
            dma((7,)), dma((7,)), dma((3,)), dma((3,)), dma, dma,
            dma((ITERS, CHUNKS, 4)), dma((ITERS, CHUNKS, 4)),
            dma((ITERS, CHUNKS)), dma((ITERS, CHUNKS)),
            dma((ITERS, 2)), dma((ITERS, 2)),
            dma((ITERS, CHUNKS, 4)), dma((ITERS, CHUNKS, 4)),
            dma((CHUNKS, 4)), dma,
            regular, regular,
        ],
        compiler_params=pltpu.CompilerParams(
            collective_id=0, has_side_effects=True, vmem_limit_bytes=48 * 1024 * 1024
        ),
    )(slot_block, mat_x, tables, estimate, pieces)


def solution(mesh):
    return jax.shard_map(
        per_device,
        mesh=mesh,
        in_specs=(
            P("blk", None, None),
            P("view", "blk", None, None),
            P("view", "blk"),
            P("view", "blk"),
            P("view", None, None),
        ),
        out_specs=P("blk", None, None),
        check_vma=False,
    )
```

```python
import functools

import jax
import jax.numpy as jnp
from jax import lax
from jax.experimental import pallas as pl
from jax.experimental.pallas import tpu as pltpu
from jax.sharding import PartitionSpec as P

ITERS = 2
HALF = 15
VIEWS = 4
SUB = 16
EDGE = 24
WIN = SUB + 2 * EDGE
CHUNKS = 4
STRIDE = 45
MESH = pl.DeviceIdType.MESH
F32 = jnp.float32
BF16 = jnp.bfloat16


def split(value):
    high = value.astype(BF16)
    low = (value - high.astype(F32)).astype(BF16)
    return high, low


def dot(a, b):
    return jnp.dot(a, b, preferred_element_type=F32)


def left_pack(weights):
    high, low = split(weights)
    return jnp.concatenate([high, high, low], axis=1)


def right_pack(weights):
    high, low = split(weights)
    top = jnp.concatenate([high, low], axis=1)
    bottom = jnp.concatenate([high, jnp.zeros_like(high)], axis=1)
    return jnp.concatenate([top, bottom], axis=0)


def from_left(packed, value):
    high, low = split(value)
    return dot(packed, jnp.concatenate([high, low, high], axis=0))


def from_right(value, packed):
    high, low = split(value)
    both = dot(jnp.concatenate([high, low], axis=1), packed)
    half = both.shape[1] // 2
    return both[:, :half] + both[:, half:]


def to_lanes(rows, depth):
    return jnp.concatenate([rows[i : i + depth] for i in range(0, rows.shape[0], depth)], axis=1)


def to_rows(lanes, width):
    return jnp.concatenate([lanes[:, i : i + width] for i in range(0, lanes.shape[1], width)], axis=0)


def kernel(
    n_blk, row_size, y_cells, z_cells,
    slot_ref, off_ref, taps_ref, est_ref, view_ref,
    out_ref,
    id_own, id_row, id_all, inv_v, inv_s,
    exch, chosen, meas,
    prm, prm_all, mxc, mxtc, wyc, wytc, wzc, wztc,
    est_half, est_flat, win, yz, stage, blurred, back_full, back_recv, corr,
    from_m1, from_p1, from_m2, from_p2, out_flat, out_half,
    id1_send, id1_recv, id2_send, id2_recv, inv_sem,
    p1_send, p1_recv, p2_send, p2_recv,
    prm_send, prm_recv, est_send, est_recv,
    halo_send, halo_recv, x_send, x_recv, b_send, b_recv, c_send, c_recv, o_send, o_recv,
    in_row, in_plane,
):
    y_half = y_cells // 2
    y_chunk = y_half // CHUNKS
    lanes = y_chunk * z_cells
    pieces, piece_rows = view_ref.shape[0], view_ref.shape[1]
    half_pieces = pieces // 2
    n_rows = n_blk // row_size
    chips = 2 * n_blk

    x = lax.axis_index("view")
    b = lax.axis_index("blk")
    a = lax.rem(b, 2)
    c = b // 2
    other = 1 - a

    def snake(q, line):
        return q + lax.rem(line, 2) * (3 - 2 * q)

    q = snake(x, c)
    n = 4 * c + q
    partner = (x, 2 * c + other)
    row, place = b // row_size, lax.rem(b, row_size)

    def along(step):
        m = lax.rem(n + step + chips, chips)
        line = m // 4
        return (snake(lax.rem(m, 4), line), 2 * line + a)

    def device(view_blk):
        return {"view": view_blk[0], "blk": view_blk[1]}

    def remote(src, dst, send, recv, where):
        return pltpu.make_async_remote_copy(
            src_ref=src, dst_ref=dst, send_sem=send, recv_sem=recv,
            device_id=device(where), device_id_type=MESH,
        )

    def await_bytes(ref, sem):
        pltpu.make_async_copy(ref, ref, sem).wait()

    taps = taps_ref[0]
    prm[...] = jnp.zeros(prm.shape, F32) + off_ref[0, 0].astype(F32)
    prm[0:3, 0 : taps.shape[1]] = taps / jnp.sum(taps, axis=1, keepdims=True)

    line_mates = []
    for step in range(1, 4):
        line_mates.append((lax.rem(x + step, 4), b))
    for step in range(4):
        line_mates.append((lax.rem(x + step, 4), 2 * c + other))
    chain = {step: along(step) for step in (-2, -1, 1, 2)}

    prm_copies = [
        remote(prm, prm_all.at[a, x], prm_send.at[i], prm_recv.at[i], mate)
        for i, mate in enumerate(line_mates)
    ]

    barrier = pltpu.get_barrier_semaphore()

    def greet_row(i, carry):
        mate = row * row_size + lax.rem(place + i, row_size)
        pl.semaphore_signal(barrier, inc=1, device_id=device((x, mate)), device_id_type=MESH)
        return carry

    def greet_column(i, carry):
        mate = lax.rem(row + i, n_rows) * row_size + place
        pl.semaphore_signal(barrier, inc=1, device_id=device((x, mate)), device_id_type=MESH)
        return carry

    lax.fori_loop(1, row_size, greet_row, 0)
    lax.fori_loop(1, n_rows, greet_column, 0)
    for mate in line_mates + list(chain.values()):
        pl.semaphore_signal(barrier, inc=1, device_id=device(mate), device_id_type=MESH)
    pl.semaphore_wait(barrier, row_size - 1 + n_rows - 1 + len(line_mates) + len(chain))

    def tell_column(i, carry):
        mate = lax.rem(row + i, n_rows) * row_size + place
        pl.semaphore_signal(in_row, inc=1, device_id=device((x, mate)), device_id_type=MESH)
        return carry

    lax.fori_loop(1, n_rows, tell_column, 0)

    id_own[...] = jnp.full(id_own.shape, slot_ref[0, 0], jnp.int32)

    def send_id(i, carry):
        mate = row * row_size + lax.rem(place + i, row_size)
        remote(id_own, id_row.at[place], id1_send, id1_recv, (x, mate)).start()
        return carry

    lax.fori_loop(1, row_size, send_id, 0)
    id_row[place] = id_own[...]

    par = q // 2
    rows_here = pl.ds(pl.multiple_of(lax.rem(q, 2) * SUB, SUB), SUB)

    def est_part(core):
        return est_ref.at[rows_here, pl.ds(pl.multiple_of(core * y_half, y_half), y_half), :]

    @pl.when(a == par)
    def _():
        remote(est_part(other), est_half, est_send, est_recv, partner).start()
        pltpu.make_async_copy(est_part(a), est_half, est_recv).start()

    for copy in prm_copies:
        copy.start()
    prm_all[a, x] = prm[...]

    pl.semaphore_wait(in_row, n_rows - 1)
    for step in range(1, 4):
        pl.semaphore_signal(
            in_plane, inc=1, device_id=device((lax.rem(x + step, 4), b)), device_id_type=MESH
        )

    def scatter(i, carry):
        to = lax.rem(b + i * STRIDE, n_blk)
        remote(view_ref.at[to], exch.at[b], p1_send, p1_recv, (x, to)).start()
        return carry

    lax.fori_loop(1, n_blk, scatter, 0)
    pltpu.make_async_copy(view_ref.at[b], exch.at[b], p1_recv).start()

    halo_plan = (
        (1, slice(EDGE, EDGE + SUB), slice(EDGE - SUB, EDGE)),
        (-1, slice(EDGE, EDGE + SUB), slice(EDGE + SUB, EDGE + 2 * SUB)),
        (2, slice(EDGE + SUB - 8, EDGE + SUB), slice(0, 8)),
        (-2, slice(EDGE, EDGE + 8), slice(WIN - 8, WIN)),
    )

    def halo_copies(it, ch):
        cols = slice(ch * lanes, (ch + 1) * lanes)
        return [
            remote(win.at[it, src, cols], win.at[it, dst, cols],
                   halo_send.at[it, ch, i], halo_recv.at[it, ch, i], chain[step])
            for i, (step, src, dst) in enumerate(halo_plan)
        ]

    corr_plan = (
        (1, slice(EDGE + SUB, EDGE + 2 * SUB), from_m1),
        (-1, slice(EDGE - SUB, EDGE), from_p1),
        (2, slice(WIN - 8, WIN), from_m2),
        (-2, slice(0, 8), from_p2),
    )

    def corr_copies(it, ch):
        cols = slice(ch * lanes, (ch + 1) * lanes)
        return [
            remote(corr.at[it, src, cols], dst.at[it, :, cols],
                   c_send.at[it, ch, i], c_recv.at[it, ch, i], chain[step])
            for i, (step, src, dst) in enumerate(corr_plan)
        ]

    await_bytes(est_half, est_recv)
    est_flat[...] = est_half[...].reshape(est_flat.shape)
    for ch in range(CHUNKS):
        for y in range(y_chunk):
            at = ch * y_chunk + y
            win[0, EDGE : EDGE + SUB, at * z_cells : (at + 1) * z_cells] = est_flat[
                pl.ds(at, SUB, stride=y_half), :
            ]
        for copy in halo_copies(0, ch):
            copy.start()

    await_bytes(id_row.at[: row_size - 1], id1_recv)
    padded = id_all.shape[1]
    sub = lax.broadcasted_iota(jnp.int32, (padded, 128), 0)
    ids = jnp.zeros((padded, 128), jnp.int32)
    for s in range(row_size):
        ids = jnp.where(sub == s, jnp.broadcast_to(id_row[s, 0:1, :], (padded, 128)), ids)
    id_all[row] = ids

    def send_row(i, carry):
        mate = lax.rem(row + i, n_rows) * row_size + place
        remote(id_all.at[row], id_all.at[row], id2_send, id2_recv, (x, mate)).start()
        return carry

    lax.fori_loop(1, n_rows, send_row, 0)

    def blur_x(it, ch):
        for copy in halo_copies(it, ch):
            copy.wait_recv()
        out = from_left(mxc[...], win[it, :, ch * lanes : (ch + 1) * lanes])
        for y in range(y_chunk):
            part = out[:, y * z_cells : (y + 1) * z_cells]
            stage[it, ch, pl.ds(y, 2 * SUB, stride=y_chunk), :] = part[2 * SUB :]
        x_copy(it, ch).start()
        for y in range(y_chunk):
            part = out[:, y * z_cells : (y + 1) * z_cells]
            yz[it, a, ch, pl.ds(y, 2 * SUB, stride=y_chunk), :] = part[: 2 * SUB]

    def x_copy(it, ch):
        return remote(
            stage.at[it, ch], yz.at[it, a, ch], x_send.at[it, ch], x_recv.at[it, ch], partner
        )

    await_bytes(id_all.at[: n_rows - 1], id2_recv)
    slot = lax.broadcasted_iota(jnp.int32, id_all.shape, 0) * row_size + lax.broadcasted_iota(
        jnp.int32, id_all.shape, 1
    )
    real = lax.broadcasted_iota(jnp.int32, id_all.shape, 1) < row_size
    hit = (id_all[...] == lax.broadcasted_iota(jnp.int32, id_all.shape, 2)) & real
    found = jnp.max(jnp.where(hit, slot, 0), axis=0)
    found = jnp.max(found, axis=0, keepdims=True)
    inv_v[...] = jnp.broadcast_to(found, inv_v.shape)
    to_scalars = pltpu.make_async_copy(inv_v, inv_s, inv_sem)
    to_scalars.start()
    to_scalars.wait()
    await_bytes(exch, p1_recv)
    pl.semaphore_wait(in_plane, 3)

    half = b // half_pieces
    meas_at = lax.rem(x, 2) * half_pieces + lax.rem(b, half_pieces)
    dst_piece = meas.at[pl.ds(pl.multiple_of(meas_at * piece_rows, 8), piece_rows), :]

    def forward(i, carry):
        j = lax.rem(b + i * STRIDE, n_blk)
        chosen[j] = exch[inv_s[0, j]]
        line = j // 2
        to_x = snake(2 * lax.rem(j, 2) + half, line)
        to_b = 2 * line + x // 2
        same = (to_x == x) & (to_b == b)

        @pl.when(same)
        def _():
            pltpu.make_async_copy(chosen.at[j], dst_piece, p2_recv).start()

        @pl.when(jnp.logical_not(same))
        def _():
            remote(chosen.at[j], dst_piece, p2_send, p2_recv, (to_x, to_b)).start()

        return carry

    lax.fori_loop(0, n_blk, forward, 0)

    for copy in prm_copies:
        copy.wait_recv()
    n_taps = taps.shape[1]
    mine, yours = 2 * a, 2 * other

    def band(shift, weights):
        value = jnp.zeros(shift.shape, F32)
        for u in range(n_taps):
            value = jnp.where(shift == u, weights[:, u : u + 1], value)
        return value

    def iota(shape, dim):
        return lax.broadcasted_iota(jnp.int32, shape, dim)

    tiles = [prm_all[par, v] for v in (mine, mine + 1, yours, yours + 1)]
    shape = (SUB, 128)
    base = iota(shape, 1) - iota(shape, 0) - (EDGE - HALF)
    mat = jnp.concatenate(
        [band(base.astype(F32) - tile[3:4, :], tile[0:1, :]) for tile in tiles], axis=0
    )
    reach = iota(mat.shape, 1) + (n * SUB - EDGE)
    mat = jnp.where((reach >= 0) & (reach < chips * SUB), mat, F32(0.0))
    mxc[...] = left_pack(mat[:, :WIN])
    mxtc[...] = left_pack(jnp.transpose(mat)[:WIN, :])
    for v in range(2):
        for cells, row, forth, back, pack in (
            (y_cells, 1, wyc, wytc, left_pack), (z_cells, 2, wztc, wzc, right_pack),
        ):
            shape = (cells, cells)
            apart = iota(shape, 1) - iota(shape, 0)
            forth[v] = pack(band(apart + HALF, tiles[v][row : row + 1, :]))
            back[v] = pack(band(HALF - apart, tiles[v][row : row + 1, :]))

    for ch in range(CHUNKS):
        blur_x(0, ch)

    group = 4

    def blur_yz(it, g):
        v = g // (SUB // group)
        rows = pl.ds(pl.multiple_of(g * (group * y_chunk), 8), group * y_chunk)
        blocks = [yz[it, h, ch, rows, :] for h in range(2) for ch in range(CHUNKS)]
        value = jnp.concatenate(
            [block[r * y_chunk : (r + 1) * y_chunk] for r in range(group) for block in blocks], axis=0
        )
        value = from_right(value, wzc[v])
        return from_left(wyc[v], to_lanes(value, y_cells))

    def back_yz(it, g, blur):
        v = g // (SUB // group)
        rows = pl.ds(pl.multiple_of(g * (group * y_cells), 8), group * y_cells)
        ratios = to_lanes(meas[rows, :], y_cells) / blur
        value = to_rows(from_left(wytc[v], ratios), z_cells)
        value = from_right(value, wztc[v])
        rows = pl.ds(pl.multiple_of(g * (group * y_half), 8), group * y_half)
        for h in range(2):
            back_full[it, h, rows, :] = jnp.concatenate(
                [value[r : r + y_half] for r in range(h * y_half, value.shape[0], y_cells)], axis=0
            )

    def back_copy(it, v):
        rows = slice(v * SUB * y_half, (v + 1) * SUB * y_half)
        return remote(
            back_full.at[it, other, rows, :], back_recv.at[it, rows, :],
            b_send.at[it, v], b_recv.at[it, v], partner,
        )

    def back_x(it, ch):
        parts = []
        for y in range(y_chunk):
            rows = pl.ds(ch * y_chunk + y, 2 * SUB, stride=y_half)
            parts.append(
                jnp.concatenate([back_full[it, a, rows, :], back_recv[it, rows, :]], axis=0)
            )
        corr[it, :, ch * lanes : (ch + 1) * lanes] = from_left(mxtc[...], jnp.concatenate(parts, axis=1))
        for copy in corr_copies(it, ch):
            copy.start()

    def updated(it, ch):
        for copy in corr_copies(it, ch):
            copy.wait_recv()
        cols = slice(ch * lanes, (ch + 1) * lanes)
        total = corr[it, EDGE : EDGE + SUB, cols] + from_m1[it, :, cols] + from_p1[it, :, cols]
        total = total + jnp.concatenate([from_m2[it, :, cols], from_p2[it, :, cols]], axis=0)
        return win[it, EDGE : EDGE + SUB, cols] * (total / VIEWS)

    def out_cols(ch, core):
        return pl.ds(pl.multiple_of(core * y_half + ch * y_chunk, 8), y_chunk)

    def out_copies(ch):
        src = out_half.at[:, ch * y_chunk : (ch + 1) * y_chunk, :]
        dst = out_ref.at[rows_here, out_cols(ch, a), :]
        own = pltpu.make_async_copy(src, dst, o_recv)
        mates = [
            remote(src, dst, o_send.at[ch, i], o_recv, (lax.rem(x + i, 4), 2 * c + par))
            for i in range(4)
        ]
        return own, mates

    for it in range(ITERS):
        for ch in range(CHUNKS):
            x_copy(it, ch).wait_recv()
        if it == 0:
            def first(g, carry):
                blurred[g] = blur_yz(0, g)
                return carry

            lax.fori_loop(0, 2 * SUB // group, first, 0)
            await_bytes(meas, p2_recv)
        per_view = SUB // group
        for v in range(2):
            def both(g, carry):
                back_yz(it, g, blurred[g] if it == 0 else blur_yz(it, g))
                return carry

            lax.fori_loop(v * per_view, (v + 1) * per_view, both, 0)
            back_copy(it, v).start()
        for v in range(2):
            back_copy(it, v).wait_recv()
        for ch in range(CHUNKS):
            back_x(it, ch)
        for ch in range(CHUNKS):
            new = updated(it, ch)
            if it + 1 < ITERS:
                win[it + 1, EDGE : EDGE + SUB, ch * lanes : (ch + 1) * lanes] = new
                for copy in halo_copies(it + 1, ch):
                    copy.start()
            else:
                for y in range(y_chunk):
                    out_flat[ch, pl.ds(y, SUB, stride=y_chunk), :] = new[
                        :, y * z_cells : (y + 1) * z_cells
                    ]
                out_half[:, ch * y_chunk : (ch + 1) * y_chunk, :] = out_flat[ch].reshape(
                    SUB, y_chunk, z_cells
                )
                own, mates = out_copies(ch)
                for mate in mates[1:]:
                    mate.start()

                @pl.when(a == par)
                def _():
                    own.start()

                @pl.when(a != par)
                def _():
                    mates[0].start()
        if it + 1 < ITERS:
            for ch in range(CHUNKS):
                blur_x(it + 1, ch)

    await_bytes(id_row.at[: row_size - 1], id1_send)
    await_bytes(id_all.at[: n_rows - 1], id2_send)
    await_bytes(exch.at[: n_blk - 1], p1_send)
    await_bytes(chosen.at[: n_blk - 1], p2_send)

    @pl.when(jnp.logical_not((a == x // 2) & (lax.rem(q, 2) == half)))
    def _():
        await_bytes(chosen.at[0], p2_send)

    @pl.when(a == par)
    def _():
        remote(est_part(other), est_half, est_send, est_recv, partner).wait_send()

    for copy in prm_copies:
        copy.wait_send()
    for it in range(ITERS):
        for ch in range(CHUNKS):
            for copy in halo_copies(it, ch) + corr_copies(it, ch) + [x_copy(it, ch)]:
                copy.wait_send()
        for v in range(2):
            back_copy(it, v).wait_send()
    for ch in range(CHUNKS):
        own, mates = out_copies(ch)
        for mate in mates[1:]:
            mate.wait_send()

        @pl.when(a != par)
        def _():
            mates[0].wait_send()

    await_bytes(out_ref, o_recv)


def per_device(estimate, view_data, slot_block, offsets, taps):
    n_blk = lax.axis_size("blk")
    block_rows, y_cells, z_cells = estimate.shape
    row_size = 16 if n_blk % 16 == 0 else n_blk // 2
    n_rows = n_blk // row_size
    padded = max(row_size, 8)
    piece_rows = block_rows * y_cells // n_blk
    pieces = view_data.reshape(n_blk, piece_rows, z_cells)
    y_half = y_cells // 2
    y_chunk = y_half // CHUNKS
    width = y_half * z_cells
    vmem = pltpu.VMEM
    dma = pltpu.SemaphoreType.DMA
    regular = pltpu.SemaphoreType.REGULAR
    return pl.pallas_call(
        functools.partial(kernel, n_blk, row_size, y_cells, z_cells),
        out_shape=jax.ShapeDtypeStruct(estimate.shape, F32),
        in_specs=[
            pl.BlockSpec(memory_space=pltpu.SMEM),
            pl.BlockSpec(memory_space=pltpu.SMEM),
            pl.BlockSpec(memory_space=pltpu.VMEM),
            pl.BlockSpec(memory_space=pl.ANY),
            pl.BlockSpec(memory_space=pl.ANY),
        ],
        out_specs=pl.BlockSpec(memory_space=pl.ANY),
        scratch_shapes=[
            vmem((8, 128), jnp.int32),
            vmem((row_size, 8, 128), jnp.int32),
            vmem((n_rows, padded, 128), jnp.int32),
            vmem((8, 128), jnp.int32),
            pltpu.SMEM((8, 128), jnp.int32),
            vmem((n_blk, piece_rows, z_cells), F32),
            vmem((n_blk, piece_rows, z_cells), F32),
            vmem((2 * SUB * y_cells, z_cells), F32),
            vmem((8, 128), F32),
            vmem((2, VIEWS, 8, 128), F32),
            vmem((4 * SUB, 3 * WIN), BF16),
            vmem((WIN, 3 * 4 * SUB), BF16),
            vmem((2, y_cells, 3 * y_cells), BF16),
            vmem((2, y_cells, 3 * y_cells), BF16),
            vmem((2, 2 * z_cells, 2 * z_cells), BF16),
            vmem((2, 2 * z_cells, 2 * z_cells), BF16),
            vmem((SUB, y_half, z_cells), F32),
            vmem((SUB * y_half, z_cells), F32),
            vmem((ITERS, WIN, width), F32),
            vmem((ITERS, 2, CHUNKS, 2 * SUB * y_chunk, z_cells), F32),
            vmem((ITERS, CHUNKS, 2 * SUB * y_chunk, z_cells), F32),
            vmem((2 * SUB // 4, y_cells, 4 * z_cells), F32),
            vmem((ITERS, 2, 2 * SUB * y_half, z_cells), F32),
            vmem((ITERS, 2 * SUB * y_half, z_cells), F32),
            vmem((ITERS, WIN, width), F32),
            vmem((ITERS, SUB, width), F32),
            vmem((ITERS, SUB, width), F32),
            vmem((ITERS, 8, width), F32),
            vmem((ITERS, 8, width), F32),
            vmem((CHUNKS, SUB * y_chunk, z_cells), F32),
            vmem((SUB, y_half, z_cells), F32),
            dma, dma, dma, dma, dma,
            dma, dma, dma, dma,
            dma((7,)), dma((7,)), dma, dma,
            dma((ITERS, CHUNKS, 4)), dma((ITERS, CHUNKS, 4)),
            dma((ITERS, CHUNKS)), dma((ITERS, CHUNKS)),
            dma((ITERS, 2)), dma((ITERS, 2)),
            dma((ITERS, CHUNKS, 4)), dma((ITERS, CHUNKS, 4)),
            dma((CHUNKS, 4)), dma,
            regular, regular,
        ],
        compiler_params=pltpu.CompilerParams(
            collective_id=0, has_side_effects=True, vmem_limit_bytes=52 * 1024 * 1024
        ),
    )(slot_block, offsets, taps, estimate, pieces)


def solution(mesh):
    return jax.shard_map(
        per_device,
        mesh=mesh,
        in_specs=(
            P("blk", None, None),
            P("view", "blk", None, None),
            P("view", "blk"),
            P("view", "blk"),
            P("view", None, None),
        ),
        out_specs=P("blk", None, None),
        check_vma=False,
    )
```

```python
import functools

import jax
import jax.numpy as jnp
from jax import lax
from jax.experimental import pallas as pl
from jax.experimental.pallas import tpu as pltpu
from jax.sharding import PartitionSpec as P

ITERS = 2
HALF = 15
VIEWS = 4
SUB = 16
EDGE = 24
WIN = SUB + 2 * EDGE
CHUNKS = 2
EARLY = 33
STRIDE = 45
MESH = pl.DeviceIdType.MESH
F32 = jnp.float32
BF16 = jnp.bfloat16


def split(value):
    high = value.astype(BF16)
    low = (value - high.astype(F32)).astype(BF16)
    return high, low


def dot(a, b):
    return jnp.dot(a, b, preferred_element_type=F32)


def left_pack(weights):
    high, low = split(weights)
    return jnp.concatenate([high, high, low], axis=1)


def right_pack(weights):
    high, low = split(weights)
    top = jnp.concatenate([high, low], axis=1)
    bottom = jnp.concatenate([high, jnp.zeros_like(high)], axis=1)
    return jnp.concatenate([top, bottom], axis=0)


def from_left(packed, value):
    high, low = split(value)
    return dot(packed, jnp.concatenate([high, low, high], axis=0))


def from_right(value, packed):
    high, low = split(value)
    both = dot(jnp.concatenate([high, low], axis=1), packed)
    half = both.shape[1] // 2
    return both[:, :half] + both[:, half:]


def to_lanes(rows, depth):
    return jnp.concatenate([rows[i : i + depth] for i in range(0, rows.shape[0], depth)], axis=1)


def to_rows(lanes, width):
    return jnp.concatenate([lanes[:, i : i + width] for i in range(0, lanes.shape[1], width)], axis=0)


def kernel(
    n_blk, row_size, y_cells, z_cells,
    slot_ref, off_ref, taps_ref, est_ref, view_ref,
    out_ref,
    id_own, id_row, id_all, inv_v, inv_s,
    exch, chosen, meas,
    prm, prm_all, mxc, mxtc, wyc, wytc, wzc, wztc,
    est_half, est_flat, win, yz, stage, blurred, back_full, back_recv, corr,
    came, merged, out_flat, out_half,
    id1_send, id1_recv, id2_send, id2_recv, inv_sem,
    p1_send, p1_recv, p2_send, p2_recv,
    prm_send, prm_recv, est_send, est_recv,
    halo_send, halo_recv, x_send, x_recv, b_send, b_recv, c_send, c_recv, o_send, f_send, o_recv,
    in_row, in_plane,
):
    y_half = y_cells // 2
    y_chunk = y_half // CHUNKS
    lanes = y_chunk * z_cells
    pieces, piece_rows = view_ref.shape[0], view_ref.shape[1]
    half_pieces = pieces // 2
    n_rows = n_blk // row_size
    chips = 2 * n_blk

    x = lax.axis_index("view")
    b = lax.axis_index("blk")
    a = lax.rem(b, 2)
    c = b // 2
    other = 1 - a

    def snake(q, line):
        return q + lax.rem(line, 2) * (3 - 2 * q)

    q = snake(x, c)
    n = 4 * c + q
    partner = (x, 2 * c + other)
    row, place = b // row_size, lax.rem(b, row_size)

    def along(step):
        m = lax.rem(n + step + chips, chips)
        line = m // 4
        return (snake(lax.rem(m, 4), line), 2 * line + a)

    last = chips - 1

    def send_along(step, copy):
        @pl.when(n != (last if step > 0 else 0))
        def _():
            copy.start()

    def sent_along(step, copy):
        @pl.when(n != (last if step > 0 else 0))
        def _():
            copy.wait_send()

    def take_along(step, copy):
        @pl.when(n != (0 if step > 0 else last))
        def _():
            copy.wait_recv()

    def device(view_blk):
        return {"view": view_blk[0], "blk": view_blk[1]}

    def remote(src, dst, send, recv, where):
        return pltpu.make_async_remote_copy(
            src_ref=src, dst_ref=dst, send_sem=send, recv_sem=recv,
            device_id=device(where), device_id_type=MESH,
        )

    def await_bytes(ref, sem):
        pltpu.make_async_copy(ref, ref, sem).wait()

    @pl.when((n == 0) | (n == last))
    def _():
        win[...] = jnp.zeros(win.shape, F32)
        came[...] = jnp.zeros(came.shape, F32)

    taps = taps_ref[0]
    prm[...] = jnp.zeros(prm.shape, F32) + off_ref[0, 0].astype(F32)
    prm[0:3, 0 : taps.shape[1]] = taps / jnp.sum(taps, axis=1, keepdims=True)

    line_mates = []
    for step in range(1, 4):
        line_mates.append((lax.rem(x + step, 4), b))
    for step in range(4):
        line_mates.append((lax.rem(x + step, 4), 2 * c + other))
    chain = {step: along(step) for step in (-1, 1)}

    prm_copies = [
        remote(prm, prm_all.at[a, x], prm_send.at[i], prm_recv.at[i], mate)
        for i, mate in enumerate(line_mates)
    ]

    barrier = pltpu.get_barrier_semaphore()

    def greet_row(i, carry):
        mate = row * row_size + lax.rem(place + i, row_size)
        pl.semaphore_signal(barrier, inc=1, device_id=device((x, mate)), device_id_type=MESH)
        return carry

    def greet_column(i, carry):
        mate = lax.rem(row + i, n_rows) * row_size + place
        pl.semaphore_signal(barrier, inc=1, device_id=device((x, mate)), device_id_type=MESH)
        return carry

    lax.fori_loop(1, row_size, greet_row, 0)
    lax.fori_loop(1, n_rows, greet_column, 0)
    for mate in line_mates:
        pl.semaphore_signal(barrier, inc=1, device_id=device(mate), device_id_type=MESH)
    pl.semaphore_wait(barrier, row_size - 1 + n_rows - 1 + len(line_mates))

    def tell_column(i, carry):
        mate = lax.rem(row + i, n_rows) * row_size + place
        pl.semaphore_signal(in_row, inc=1, device_id=device((x, mate)), device_id_type=MESH)
        return carry

    lax.fori_loop(1, n_rows, tell_column, 0)

    id_own[...] = jnp.full(id_own.shape, slot_ref[0, 0], jnp.int32)

    def send_id(i, carry):
        mate = row * row_size + lax.rem(place + i, row_size)
        remote(id_own, id_row.at[place], id1_send, id1_recv, (x, mate)).start()
        return carry

    lax.fori_loop(1, row_size, send_id, 0)
    id_row[place] = id_own[...]

    par = q // 2
    rows_here = pl.ds(pl.multiple_of(lax.rem(q, 2) * SUB, SUB), SUB)

    def est_part(core):
        return est_ref.at[rows_here, pl.ds(pl.multiple_of(core * y_half, y_half), y_half), :]

    @pl.when(a == par)
    def _():
        remote(est_part(other), est_half, est_send, est_recv, partner).start()
        pltpu.make_async_copy(est_part(a), est_half, est_recv).start()

    for copy in prm_copies:
        copy.start()
    prm_all[a, x] = prm[...]

    pl.semaphore_wait(in_row, n_rows - 1)
    for step in range(1, 4):
        pl.semaphore_signal(
            in_plane, inc=1, device_id=device((lax.rem(x + step, 4), b)), device_id_type=MESH
        )

    def scatter(i, carry):
        to = lax.rem(b + i * STRIDE, n_blk)
        remote(view_ref.at[to], exch.at[b], p1_send, p1_recv, (x, to)).start()
        return carry

    early = min(EARLY, n_blk)
    lax.fori_loop(1, early, scatter, 0)

    halo_plan = (
        (1, EDGE + 8, EDGE - 8), (-1, EDGE, EDGE + SUB),
        (1, EDGE, EDGE - SUB), (-1, EDGE + 8, EDGE + SUB + 8),
        (1, EDGE - 8, 0), (-1, EDGE + SUB, WIN - 8),
    )

    def halo_copies(it, ch):
        cols = slice(ch * lanes, (ch + 1) * lanes)
        return [
            remote(win.at[it, src : src + 8, cols], win.at[it, dst : dst + 8, cols],
                   halo_send.at[it, ch, i], halo_recv.at[it, ch, i], chain[step])
            for i, (step, src, dst) in enumerate(halo_plan)
        ]

    def pass_on(it, ch):
        copies = halo_copies(it, ch)
        for i in range(2):
            step = halo_plan[i][0]
            take_along(step, copies[i])
            send_along(step, copies[4 + i])

    corr_plan = (
        (1, WIN - 8), (-1, 0),
        (1, EDGE + SUB + 8), (-1, EDGE - SUB),
        (1, EDGE + SUB), (-1, EDGE - 8),
    )

    def corr_copies(it, ch):
        cols = slice(ch * lanes, (ch + 1) * lanes)
        copies = []
        for i, (step, src) in enumerate(corr_plan):
            here = corr.at[it, src : src + 8, cols] if i < 4 else merged.at[it, i - 4, :, cols]
            copies.append(
                remote(here, came.at[it, i, :, cols], c_send.at[it, ch, i], c_recv.at[it, ch, i], chain[step])
            )
        return copies

    def merge(it, ch):
        cols = slice(ch * lanes, (ch + 1) * lanes)
        copies = corr_copies(it, ch)
        for i in range(2):
            step, src = corr_plan[4 + i]
            take_along(step, copies[i])
            merged[it, i, :, cols] = corr[it, src : src + 8, cols] + came[it, i, :, cols]
            send_along(step, copies[4 + i])

    await_bytes(est_half, est_recv)
    est_flat[...] = est_half[...].reshape(est_flat.shape)
    for ch in range(CHUNKS):
        for y in range(y_chunk):
            at = ch * y_chunk + y
            win[0, EDGE : EDGE + SUB, at * z_cells : (at + 1) * z_cells] = est_flat[
                pl.ds(at, SUB, stride=y_half), :
            ]
        for i, copy in enumerate(halo_copies(0, ch)[:4]):
            send_along(halo_plan[i][0], copy)

    lax.fori_loop(early, n_blk, scatter, 0)
    pltpu.make_async_copy(view_ref.at[b], exch.at[b], p1_recv).start()

    await_bytes(id_row.at[: row_size - 1], id1_recv)
    padded = id_all.shape[1]
    sub = lax.broadcasted_iota(jnp.int32, (padded, 128), 0)
    ids = jnp.zeros((padded, 128), jnp.int32)
    for s in range(row_size):
        ids = jnp.where(sub == s, jnp.broadcast_to(id_row[s, 0:1, :], (padded, 128)), ids)
    id_all[row] = ids

    def send_row(i, carry):
        mate = lax.rem(row + i, n_rows) * row_size + place
        remote(id_all.at[row], id_all.at[row], id2_send, id2_recv, (x, mate)).start()
        return carry

    lax.fori_loop(1, n_rows, send_row, 0)

    def blur_x(it, ch):
        for i, copy in enumerate(halo_copies(it, ch)[2:]):
            take_along(halo_plan[2 + i][0], copy)
        out = from_left(mxc[...], win[it, :, ch * lanes : (ch + 1) * lanes])
        for y in range(y_chunk):
            part = out[:, y * z_cells : (y + 1) * z_cells]
            stage[it, ch, pl.ds(y, 2 * SUB, stride=y_chunk), :] = part[2 * SUB :]
        x_copy(it, ch).start()
        for y in range(y_chunk):
            part = out[:, y * z_cells : (y + 1) * z_cells]
            yz[it, a, ch, pl.ds(y, 2 * SUB, stride=y_chunk), :] = part[: 2 * SUB]

    def x_copy(it, ch):
        return remote(
            stage.at[it, ch], yz.at[it, a, ch], x_send.at[it, ch], x_recv.at[it, ch], partner
        )

    for copy in prm_copies:
        copy.wait_recv()
    n_taps = taps.shape[1]
    mine, yours = 2 * a, 2 * other

    def band(shift, weights):
        value = jnp.zeros(shift.shape, F32)
        for u in range(n_taps):
            value = jnp.where(shift == u, weights[:, u : u + 1], value)
        return value

    def iota(shape, dim):
        return lax.broadcasted_iota(jnp.int32, shape, dim)

    tiles = [prm_all[par, v] for v in (mine, mine + 1, yours, yours + 1)]
    shape = (SUB, 128)
    base = iota(shape, 1) - iota(shape, 0) - (EDGE - HALF)
    mat = jnp.concatenate(
        [band(base.astype(F32) - tile[3:4, :], tile[0:1, :]) for tile in tiles], axis=0
    )
    reach = iota(mat.shape, 1) + (n * SUB - EDGE)
    mat = jnp.where((reach >= 0) & (reach < chips * SUB), mat, F32(0.0))
    mxc[...] = left_pack(mat[:, :WIN])
    mxtc[...] = left_pack(jnp.transpose(mat)[:WIN, :])
    for v in range(2):
        for cells, row, forth, back, pack in (
            (y_cells, 1, wyc, wytc, left_pack), (z_cells, 2, wztc, wzc, right_pack),
        ):
            shape = (cells, cells)
            apart = iota(shape, 1) - iota(shape, 0)
            forth[v] = pack(band(apart + HALF, tiles[v][row : row + 1, :]))
            back[v] = pack(band(HALF - apart, tiles[v][row : row + 1, :]))

    for ch in range(CHUNKS):
        pass_on(0, ch)
    for ch in range(CHUNKS):
        blur_x(0, ch)

    await_bytes(id_all.at[: n_rows - 1], id2_recv)
    slot = lax.broadcasted_iota(jnp.int32, id_all.shape, 0) * row_size + lax.broadcasted_iota(
        jnp.int32, id_all.shape, 1
    )
    real = lax.broadcasted_iota(jnp.int32, id_all.shape, 1) < row_size
    hit = (id_all[...] == lax.broadcasted_iota(jnp.int32, id_all.shape, 2)) & real
    found = jnp.max(jnp.where(hit, slot, 0), axis=0)
    found = jnp.max(found, axis=0, keepdims=True)
    inv_v[...] = jnp.broadcast_to(found, inv_v.shape)
    to_scalars = pltpu.make_async_copy(inv_v, inv_s, inv_sem)
    to_scalars.start()
    to_scalars.wait()
    await_bytes(exch, p1_recv)
    pl.semaphore_wait(in_plane, 3)

    half = b // half_pieces
    meas_at = lax.rem(x, 2) * half_pieces + lax.rem(b, half_pieces)
    dst_piece = meas.at[pl.ds(pl.multiple_of(meas_at * piece_rows, 8), piece_rows), :]

    def forward(i, carry):
        j = lax.rem(b + i * STRIDE, n_blk)
        chosen[j] = exch[inv_s[0, j]]
        line = j // 2
        to_x = snake(2 * lax.rem(j, 2) + half, line)
        to_b = 2 * line + x // 2
        same = (to_x == x) & (to_b == b)

        @pl.when(same)
        def _():
            pltpu.make_async_copy(chosen.at[j], dst_piece, p2_recv).start()

        @pl.when(jnp.logical_not(same))
        def _():
            remote(chosen.at[j], dst_piece, p2_send, p2_recv, (to_x, to_b)).start()

        return carry

    lax.fori_loop(0, n_blk, forward, 0)

    group = 4

    def blur_yz(it, g):
        v = g // (SUB // group)
        rows = pl.ds(pl.multiple_of(g * (group * y_chunk), 8), group * y_chunk)
        blocks = [yz[it, h, ch, rows, :] for h in range(2) for ch in range(CHUNKS)]
        value = jnp.concatenate(
            [block[r * y_chunk : (r + 1) * y_chunk] for r in range(group) for block in blocks], axis=0
        )
        value = from_right(value, wzc[v])
        return from_left(wyc[v], to_lanes(value, y_cells))

    def back_yz(it, g, blur):
        v = g // (SUB // group)
        rows = pl.ds(pl.multiple_of(g * (group * y_cells), 8), group * y_cells)
        ratios = to_lanes(meas[rows, :], y_cells) / blur
        value = to_rows(from_left(wytc[v], ratios), z_cells)
        value = from_right(value, wztc[v])
        rows = pl.ds(pl.multiple_of(g * (group * y_half), 8), group * y_half)
        for h in range(2):
            back_full[it, h, rows, :] = jnp.concatenate(
                [value[r : r + y_half] for r in range(h * y_half, value.shape[0], y_cells)], axis=0
            )

    def back_copy(it, v):
        rows = slice(v * SUB * y_half, (v + 1) * SUB * y_half)
        return remote(
            back_full.at[it, other, rows, :], back_recv.at[it, rows, :],
            b_send.at[it, v], b_recv.at[it, v], partner,
        )

    def back_x(it, ch):
        parts = []
        for y in range(y_chunk):
            rows = pl.ds(ch * y_chunk + y, 2 * SUB, stride=y_half)
            parts.append(
                jnp.concatenate([back_full[it, a, rows, :], back_recv[it, rows, :]], axis=0)
            )
        corr[it, :, ch * lanes : (ch + 1) * lanes] = from_left(mxtc[...], jnp.concatenate(parts, axis=1))
        for i, copy in enumerate(corr_copies(it, ch)[:4]):
            send_along(corr_plan[i][0], copy)

    def updated(it, ch):
        for i, copy in enumerate(corr_copies(it, ch)[2:]):
            take_along(corr_plan[2 + i][0], copy)
        cols = slice(ch * lanes, (ch + 1) * lanes)
        total = corr[it, EDGE : EDGE + SUB, cols] + jnp.concatenate([
            came[it, 4, :, cols] + came[it, 3, :, cols],
            came[it, 2, :, cols] + came[it, 5, :, cols],
        ], axis=0)
        return win[it, EDGE : EDGE + SUB, cols] * (total / VIEWS)

    def out_cols(ch, core):
        return pl.ds(pl.multiple_of(core * y_half + ch * y_chunk, 8), y_chunk)

    def out_copies(ch):
        src = out_half.at[:, ch * y_chunk : (ch + 1) * y_chunk, :]
        dst = out_ref.at[rows_here, out_cols(ch, a), :]
        own = pltpu.make_async_copy(src, dst, o_recv.at[ch, a, 0])
        mates = [
            remote(src, dst, o_send.at[ch, i], o_recv.at[ch, a, min(i, 1)], (to_x, 2 * c + par))
            for i, to_x in enumerate((x, lax.rem(x + 1, 4), lax.rem(x + 3, 4)))
        ]
        return own, mates

    flip = lax.rem(c, 2)
    odd = lax.rem(x + 1 - flip, 2)
    ahead = lax.rem(x - snake(2 * a + odd, c) + 4, 4)
    onward = lax.rem(x + 2 - ahead + 4, 4)
    onward_rows = pl.ds(odd * SUB + 8 * (ahead // 2), 8)
    odd_rows = pl.ds(odd * SUB, SUB)

    def onward_copies(ch):
        copies = []
        for h in range(2):
            part = out_ref.at[onward_rows, out_cols(ch, h), :]
            copies.append(remote(part, part, f_send.at[ch, h], o_recv.at[ch, h, 0], (onward, b)))
        return copies

    def send_on(ch):
        for h, copy in enumerate(onward_copies(ch)):
            await_bytes(out_ref.at[odd_rows, out_cols(ch, h), :], o_recv.at[ch, h, 1])
            copy.start()

    for it in range(ITERS):
        for ch in range(CHUNKS):
            x_copy(it, ch).wait_recv()
        if it == 0:
            def first(g, carry):
                blurred[g] = blur_yz(0, g)
                return carry

            lax.fori_loop(0, 2 * SUB // group, first, 0)
            await_bytes(meas, p2_recv)
        per_view = SUB // group
        for v in range(2):
            def both(g, carry):
                back_yz(it, g, blurred[g] if it == 0 else blur_yz(it, g))
                return carry

            lax.fori_loop(v * per_view, (v + 1) * per_view, both, 0)
            back_copy(it, v).start()
        for v in range(2):
            back_copy(it, v).wait_recv()
        for ch in range(CHUNKS):
            back_x(it, ch)
        def finish(ch):
            new = updated(it, ch)
            if it + 1 < ITERS:
                win[it + 1, EDGE : EDGE + SUB, ch * lanes : (ch + 1) * lanes] = new
                for i, copy in enumerate(halo_copies(it + 1, ch)[:4]):
                    send_along(halo_plan[i][0], copy)
                return
            for y in range(y_chunk):
                out_flat[ch, pl.ds(y, SUB, stride=y_chunk), :] = new[
                    :, y * z_cells : (y + 1) * z_cells
                ]
            out_half[:, ch * y_chunk : (ch + 1) * y_chunk, :] = out_flat[ch].reshape(
                SUB, y_chunk, z_cells
            )
            own, mates = out_copies(ch)
            for mate in mates[1:]:
                mate.start()

            @pl.when(a == par)
            def _():
                own.start()

            @pl.when(a != par)
            def _():
                mates[0].start()

        def move_on(ch):
            if it + 1 < ITERS:
                pass_on(it + 1, ch)
            else:
                send_on(ch)

        for t in range(CHUNKS + 3):
            if t < CHUNKS:
                merge(it, t)
            if 0 <= t - 1 < CHUNKS:
                finish(t - 1)
            if 0 <= t - 2 < CHUNKS:
                move_on(t - 2)
            if 0 <= t - 3 < CHUNKS and it + 1 < ITERS:
                blur_x(it + 1, t - 3)

    await_bytes(id_row.at[: row_size - 1], id1_send)
    await_bytes(id_all.at[: n_rows - 1], id2_send)
    await_bytes(exch.at[: n_blk - 1], p1_send)
    await_bytes(chosen.at[: n_blk - 1], p2_send)

    @pl.when(jnp.logical_not((a == x // 2) & (lax.rem(q, 2) == half)))
    def _():
        await_bytes(chosen.at[0], p2_send)

    @pl.when(a == par)
    def _():
        remote(est_part(other), est_half, est_send, est_recv, partner).wait_send()

    for copy in prm_copies:
        copy.wait_send()
    for it in range(ITERS):
        for ch in range(CHUNKS):
            for i in range(6):
                sent_along(halo_plan[i][0], halo_copies(it, ch)[i])
                sent_along(corr_plan[i][0], corr_copies(it, ch)[i])
            x_copy(it, ch).wait_send()
        for v in range(2):
            back_copy(it, v).wait_send()
    for ch in range(CHUNKS):
        own, mates = out_copies(ch)
        for copy in mates[1:] + onward_copies(ch):
            copy.wait_send()

        @pl.when(a != par)
        def _():
            mates[0].wait_send()

        for h in range(2):
            await_bytes(out_half.at[:, :y_chunk, :], o_recv.at[ch, h, 0])


def per_device(estimate, view_data, slot_block, offsets, taps):
    n_blk = lax.axis_size("blk")
    block_rows, y_cells, z_cells = estimate.shape
    row_size = 16 if n_blk % 16 == 0 else n_blk // 2
    n_rows = n_blk // row_size
    padded = max(row_size, 8)
    piece_rows = block_rows * y_cells // n_blk
    pieces = view_data.reshape(n_blk, piece_rows, z_cells)
    y_half = y_cells // 2
    y_chunk = y_half // CHUNKS
    width = y_half * z_cells
    vmem = pltpu.VMEM
    dma = pltpu.SemaphoreType.DMA
    regular = pltpu.SemaphoreType.REGULAR
    return pl.pallas_call(
        functools.partial(kernel, n_blk, row_size, y_cells, z_cells),
        out_shape=jax.ShapeDtypeStruct(estimate.shape, F32),
        in_specs=[
            pl.BlockSpec(memory_space=pltpu.SMEM),
            pl.BlockSpec(memory_space=pltpu.SMEM),
            pl.BlockSpec(memory_space=pltpu.VMEM),
            pl.BlockSpec(memory_space=pl.ANY),
            pl.BlockSpec(memory_space=pl.ANY),
        ],
        out_specs=pl.BlockSpec(memory_space=pl.ANY),
        scratch_shapes=[
            vmem((8, 128), jnp.int32),
            vmem((row_size, 8, 128), jnp.int32),
            vmem((n_rows, padded, 128), jnp.int32),
            vmem((8, 128), jnp.int32),
            pltpu.SMEM((8, 128), jnp.int32),
            vmem((n_blk, piece_rows, z_cells), F32),
            vmem((n_blk, piece_rows, z_cells), F32),
            vmem((2 * SUB * y_cells, z_cells), F32),
            vmem((8, 128), F32),
            vmem((2, VIEWS, 8, 128), F32),
            vmem((4 * SUB, 3 * WIN), BF16),
            vmem((WIN, 3 * 4 * SUB), BF16),
            vmem((2, y_cells, 3 * y_cells), BF16),
            vmem((2, y_cells, 3 * y_cells), BF16),
            vmem((2, 2 * z_cells, 2 * z_cells), BF16),
            vmem((2, 2 * z_cells, 2 * z_cells), BF16),
            vmem((SUB, y_half, z_cells), F32),
            vmem((SUB * y_half, z_cells), F32),
            vmem((ITERS, WIN, width), F32),
            vmem((ITERS, 2, CHUNKS, 2 * SUB * y_chunk, z_cells), F32),
            vmem((ITERS, CHUNKS, 2 * SUB * y_chunk, z_cells), F32),
            vmem((2 * SUB // 4, y_cells, 4 * z_cells), F32),
            vmem((ITERS, 2, 2 * SUB * y_half, z_cells), F32),
            vmem((ITERS, 2 * SUB * y_half, z_cells), F32),
            vmem((ITERS, WIN, width), F32),
            vmem((ITERS, 6, 8, width), F32),
            vmem((ITERS, 2, 8, width), F32),
            vmem((CHUNKS, SUB * y_chunk, z_cells), F32),
            vmem((SUB, y_half, z_cells), F32),
            dma, dma, dma, dma, dma,
            dma, dma, dma, dma,
            dma((7,)), dma((7,)), dma, dma,
            dma((ITERS, CHUNKS, 6)), dma((ITERS, CHUNKS, 6)),
            dma((ITERS, CHUNKS)), dma((ITERS, CHUNKS)),
            dma((ITERS, 2)), dma((ITERS, 2)),
            dma((ITERS, CHUNKS, 6)), dma((ITERS, CHUNKS, 6)),
            dma((CHUNKS, 3)), dma((CHUNKS, 2)), dma((CHUNKS, 2, 2)),
            regular, regular,
        ],
        compiler_params=pltpu.CompilerParams(
            collective_id=0, has_side_effects=True, vmem_limit_bytes=52 * 1024 * 1024
        ),
    )(slot_block, offsets, taps, estimate, pieces)


def solution(mesh):
    return jax.shard_map(
        per_device,
        mesh=mesh,
        in_specs=(
            P("blk", None, None),
            P("view", "blk", None, None),
            P("view", "blk"),
            P("view", "blk"),
            P("view", None, None),
        ),
        out_specs=P("blk", None, None),
        check_vma=False,
    )
```

```python
import functools

import jax
import jax.numpy as jnp
from jax import lax
from jax.experimental import pallas as pl
from jax.experimental.pallas import tpu as pltpu
from jax.sharding import PartitionSpec as P

ITERS = 2
HALF = 15
VIEWS = 4
SUB = 16
EDGE = 24
WIN = SUB + 2 * EDGE
CHUNKS = 2
EARLY = 33
STRIDE = 45
MESH = pl.DeviceIdType.MESH
F32 = jnp.float32
BF16 = jnp.bfloat16


def split(value):
    high = value.astype(BF16)
    low = (value - high.astype(F32)).astype(BF16)
    return high, low


def dot(a, b):
    return jnp.dot(a, b, preferred_element_type=F32)


def left_pack(weights):
    high, low = split(weights)
    return jnp.concatenate([high, high, low], axis=1)


def right_pack(weights):
    high, low = split(weights)
    top = jnp.concatenate([high, low], axis=1)
    bottom = jnp.concatenate([high, jnp.zeros_like(high)], axis=1)
    return jnp.concatenate([top, bottom], axis=0)


def from_left(packed, value):
    high, low = split(value)
    return dot(packed, jnp.concatenate([high, low, high], axis=0))


def from_right(value, packed):
    high, low = split(value)
    both = dot(jnp.concatenate([high, low], axis=1), packed)
    half = both.shape[1] // 2
    return both[:, :half] + both[:, half:]


def to_lanes(rows, depth):
    return jnp.concatenate([rows[i : i + depth] for i in range(0, rows.shape[0], depth)], axis=1)


def to_rows(lanes, width):
    return jnp.concatenate([lanes[:, i : i + width] for i in range(0, lanes.shape[1], width)], axis=0)


def kernel(
    n_blk, row_size, y_cells, z_cells,
    slot_ref, off_ref, taps_ref, est_ref, view_ref,
    out_ref,
    id_own, id_row, id_all, inv_v, inv_s,
    exch, chosen, meas,
    prm, prm_all, mxc, mxtc, wyc, wytc, wzc, wztc,
    est_half, est_flat, win, yz, stage, blurred, back_full, back_recv, corr,
    came, merged, out_flat, out_half,
    id1_send, id1_recv, id2_send, id2_recv, inv_sem,
    p1_send, p1_recv, p2_send, p2_recv,
    prm_send, prm_recv, est_send, est_recv,
    halo_send, halo_recv, x_send, x_recv, b_send, b_recv, c_send, c_recv, o_send, f_send, o_recv,
    in_row, in_plane,
):
    y_half = y_cells // 2
    y_chunk = y_half // CHUNKS
    lanes = y_chunk * z_cells
    pieces, piece_rows = view_ref.shape[0], view_ref.shape[1]
    half_pieces = pieces // 2
    n_rows = n_blk // row_size
    chips = 2 * n_blk

    x = lax.axis_index("view")
    b = lax.axis_index("blk")
    a = lax.rem(b, 2)
    c = b // 2
    other = 1 - a

    def snake(q, line):
        return q + lax.rem(line, 2) * (3 - 2 * q)

    q = snake(x, c)
    n = 4 * c + q
    partner = (x, 2 * c + other)
    row, place = b // row_size, lax.rem(b, row_size)

    def along(step):
        m = lax.rem(n + step + chips, chips)
        line = m // 4
        return (snake(lax.rem(m, 4), line), 2 * line + a)

    last = chips - 1

    def send_along(step, copy):
        @pl.when(n != (last if step > 0 else 0))
        def _():
            copy.start()

    def sent_along(step, copy):
        @pl.when(n != (last if step > 0 else 0))
        def _():
            copy.wait_send()

    def take_along(step, copy):
        @pl.when(n != (0 if step > 0 else last))
        def _():
            copy.wait_recv()

    def device(view_blk):
        return {"view": view_blk[0], "blk": view_blk[1]}

    def remote(src, dst, send, recv, where):
        return pltpu.make_async_remote_copy(
            src_ref=src, dst_ref=dst, send_sem=send, recv_sem=recv,
            device_id=device(where), device_id_type=MESH,
        )

    def await_bytes(ref, sem):
        pltpu.make_async_copy(ref, ref, sem).wait()

    @pl.when((n == 0) | (n == last))
    def _():
        win[...] = jnp.zeros(win.shape, F32)
        came[...] = jnp.zeros(came.shape, F32)

    taps = taps_ref[0]
    prm[...] = jnp.zeros(prm.shape, F32) + off_ref[0, 0].astype(F32)
    prm[0:3, 0 : taps.shape[1]] = taps / jnp.sum(taps, axis=1, keepdims=True)

    line_mates = []
    for step in range(1, 4):
        line_mates.append((lax.rem(x + step, 4), b))
    for step in range(4):
        line_mates.append((lax.rem(x + step, 4), 2 * c + other))
    chain = {step: along(step) for step in (-1, 1)}

    prm_copies = [
        remote(prm, prm_all.at[a, x], prm_send.at[i], prm_recv.at[i], mate)
        for i, mate in enumerate(line_mates)
    ]

    barrier = pltpu.get_barrier_semaphore()

    def greet_row(i, carry):
        mate = row * row_size + lax.rem(place + i, row_size)
        pl.semaphore_signal(barrier, inc=1, device_id=device((x, mate)), device_id_type=MESH)
        return carry

    def greet_column(i, carry):
        mate = lax.rem(row + i, n_rows) * row_size + place
        pl.semaphore_signal(barrier, inc=1, device_id=device((x, mate)), device_id_type=MESH)
        return carry

    lax.fori_loop(1, row_size, greet_row, 0)
    lax.fori_loop(1, n_rows, greet_column, 0)
    for mate in line_mates:
        pl.semaphore_signal(barrier, inc=1, device_id=device(mate), device_id_type=MESH)
    pl.semaphore_wait(barrier, row_size - 1 + n_rows - 1 + len(line_mates))

    def tell_column(i, carry):
        mate = lax.rem(row + i, n_rows) * row_size + place
        pl.semaphore_signal(in_row, inc=1, device_id=device((x, mate)), device_id_type=MESH)
        return carry

    lax.fori_loop(1, n_rows, tell_column, 0)

    id_own[...] = jnp.full(id_own.shape, slot_ref[0, 0], jnp.int32)

    def send_id(i, carry):
        mate = row * row_size + lax.rem(place + i, row_size)
        remote(id_own, id_row.at[place], id1_send, id1_recv, (x, mate)).start()
        return carry

    lax.fori_loop(1, row_size, send_id, 0)
    id_row[place] = id_own[...]

    par = q // 2
    rows_here = pl.ds(pl.multiple_of(lax.rem(q, 2) * SUB, SUB), SUB)

    def est_part(core):
        return est_ref.at[rows_here, pl.ds(pl.multiple_of(core * y_half, y_half), y_half), :]

    @pl.when(a == par)
    def _():
        remote(est_part(other), est_half, est_send, est_recv, partner).start()
        pltpu.make_async_copy(est_part(a), est_half, est_recv).start()

    for copy in prm_copies:
        copy.start()
    prm_all[a, x] = prm[...]

    pl.semaphore_wait(in_row, n_rows - 1)
    for step in range(1, 4):
        pl.semaphore_signal(
            in_plane, inc=1, device_id=device((lax.rem(x + step, 4), b)), device_id_type=MESH
        )

    def scatter(i, carry):
        to = lax.rem(b + i * STRIDE, n_blk)
        remote(view_ref.at[to], exch.at[b], p1_send, p1_recv, (x, to)).start()
        return carry

    early = min(EARLY, n_blk)
    lax.fori_loop(1, early, scatter, 0)

    halo_plan = (
        (1, EDGE + 8, EDGE - 8), (-1, EDGE, EDGE + SUB),
        (1, EDGE, EDGE - SUB), (-1, EDGE + 8, EDGE + SUB + 8),
        (1, EDGE - 8, 0), (-1, EDGE + SUB, WIN - 8),
    )

    def halo_copies(it, ch):
        cols = slice(ch * lanes, (ch + 1) * lanes)
        return [
            remote(win.at[it, src : src + 8, cols], win.at[it, dst : dst + 8, cols],
                   halo_send.at[it, ch, i], halo_recv.at[it, ch, i], chain[step])
            for i, (step, src, dst) in enumerate(halo_plan)
        ]

    def pass_on(it, ch):
        copies = halo_copies(it, ch)
        for i in range(2):
            step = halo_plan[i][0]
            take_along(step, copies[i])
            send_along(step, copies[4 + i])

    corr_plan = (
        (1, WIN - 8), (-1, 0),
        (1, EDGE + SUB + 8), (-1, EDGE - SUB),
        (1, EDGE + SUB), (-1, EDGE - 8),
    )

    def corr_copies(it, ch):
        cols = slice(ch * lanes, (ch + 1) * lanes)
        copies = []
        for i, (step, src) in enumerate(corr_plan):
            here = corr.at[it, src : src + 8, cols] if i < 4 else merged.at[it, i - 4, :, cols]
            copies.append(
                remote(here, came.at[it, i, :, cols], c_send.at[it, ch, i], c_recv.at[it, ch, i], chain[step])
            )
        return copies

    def merge(it, ch):
        cols = slice(ch * lanes, (ch + 1) * lanes)
        copies = corr_copies(it, ch)
        for i in range(2):
            step, src = corr_plan[4 + i]
            take_along(step, copies[i])
            merged[it, i, :, cols] = corr[it, src : src + 8, cols] + came[it, i, :, cols]
            send_along(step, copies[4 + i])

    await_bytes(est_half, est_recv)
    est_flat[...] = est_half[...].reshape(est_flat.shape)
    for ch in range(CHUNKS):
        for y in range(y_chunk):
            at = ch * y_chunk + y
            win[0, EDGE : EDGE + SUB, at * z_cells : (at + 1) * z_cells] = est_flat[
                pl.ds(at, SUB, stride=y_half), :
            ]
        for i, copy in enumerate(halo_copies(0, ch)[:4]):
            send_along(halo_plan[i][0], copy)

    lax.fori_loop(early, n_blk, scatter, 0)
    pltpu.make_async_copy(view_ref.at[b], exch.at[b], p1_recv).start()

    await_bytes(id_row.at[: row_size - 1], id1_recv)
    padded = id_all.shape[1]
    sub = lax.broadcasted_iota(jnp.int32, (padded, 128), 0)
    ids = jnp.zeros((padded, 128), jnp.int32)
    for s in range(row_size):
        ids = jnp.where(sub == s, jnp.broadcast_to(id_row[s, 0:1, :], (padded, 128)), ids)
    id_all[row] = ids

    def send_row(i, carry):
        mate = lax.rem(row + i, n_rows) * row_size + place
        remote(id_all.at[row], id_all.at[row], id2_send, id2_recv, (x, mate)).start()
        return carry

    lax.fori_loop(1, n_rows, send_row, 0)

    def blur_x(it, ch):
        for i, copy in enumerate(halo_copies(it, ch)[2:]):
            take_along(halo_plan[2 + i][0], copy)
        out = from_left(mxc[...], win[it, :, ch * lanes : (ch + 1) * lanes])
        for y in range(y_chunk):
            part = out[:, y * z_cells : (y + 1) * z_cells]
            stage[it, ch, pl.ds(y, 2 * SUB, stride=y_chunk), :] = part[2 * SUB :]
        x_copy(it, ch).start()
        for y in range(y_chunk):
            part = out[:, y * z_cells : (y + 1) * z_cells]
            yz[it, a, ch, pl.ds(y, 2 * SUB, stride=y_chunk), :] = part[: 2 * SUB]

    def x_copy(it, ch):
        return remote(
            stage.at[it, ch], yz.at[it, a, ch], x_send.at[it, ch], x_recv.at[it, ch], partner
        )

    for copy in prm_copies:
        copy.wait_recv()
    n_taps = taps.shape[1]
    mine, yours = 2 * a, 2 * other

    def band(shift, weights):
        value = jnp.zeros(shift.shape, F32)
        for u in range(n_taps):
            value = jnp.where(shift == u, weights[:, u : u + 1], value)
        return value

    def iota(shape, dim):
        return lax.broadcasted_iota(jnp.int32, shape, dim)

    tiles = [prm_all[par, v] for v in (mine, mine + 1, yours, yours + 1)]
    shape = (SUB, 128)
    base = iota(shape, 1) - iota(shape, 0) - (EDGE - HALF)
    mat = jnp.concatenate(
        [band(base.astype(F32) - tile[3:4, :], tile[0:1, :]) for tile in tiles], axis=0
    )
    reach = iota(mat.shape, 1) + (n * SUB - EDGE)
    mat = jnp.where((reach >= 0) & (reach < chips * SUB), mat, F32(0.0))
    mxc[...] = left_pack(mat[:, :WIN])
    mxtc[...] = left_pack(jnp.transpose(mat)[:WIN, :])
    for v in range(2):
        for cells, row, forth, back, pack in (
            (y_cells, 1, wyc, wytc, left_pack), (z_cells, 2, wztc, wzc, right_pack),
        ):
            shape = (cells, cells)
            apart = iota(shape, 1) - iota(shape, 0)
            forth[v] = pack(band(apart + HALF, tiles[v][row : row + 1, :]))
            back[v] = pack(band(HALF - apart, tiles[v][row : row + 1, :]))

    for ch in range(CHUNKS):
        pass_on(0, ch)
    for ch in range(CHUNKS):
        blur_x(0, ch)

    await_bytes(id_all.at[: n_rows - 1], id2_recv)
    slot = lax.broadcasted_iota(jnp.int32, id_all.shape, 0) * row_size + lax.broadcasted_iota(
        jnp.int32, id_all.shape, 1
    )
    real = lax.broadcasted_iota(jnp.int32, id_all.shape, 1) < row_size
    hit = (id_all[...] == lax.broadcasted_iota(jnp.int32, id_all.shape, 2)) & real
    found = jnp.max(jnp.where(hit, slot, 0), axis=0)
    found = jnp.max(found, axis=0, keepdims=True)
    inv_v[...] = jnp.broadcast_to(found, inv_v.shape)
    to_scalars = pltpu.make_async_copy(inv_v, inv_s, inv_sem)
    to_scalars.start()
    to_scalars.wait()
    await_bytes(exch, p1_recv)
    pl.semaphore_wait(in_plane, 3)

    half = b // half_pieces
    meas_at = lax.rem(x, 2) * half_pieces + lax.rem(b, half_pieces)
    dst_piece = meas.at[pl.ds(pl.multiple_of(meas_at * piece_rows, 8), piece_rows), :]

    def forward(i, carry):
        j = lax.rem(b + i * STRIDE, n_blk)
        chosen[j] = exch[inv_s[0, j]]
        line = j // 2
        to_x = snake(2 * lax.rem(j, 2) + half, line)
        to_b = 2 * line + x // 2
        same = (to_x == x) & (to_b == b)

        @pl.when(same)
        def _():
            pltpu.make_async_copy(chosen.at[j], dst_piece, p2_recv).start()

        @pl.when(jnp.logical_not(same))
        def _():
            remote(chosen.at[j], dst_piece, p2_send, p2_recv, (to_x, to_b)).start()

        return carry

    lax.fori_loop(0, n_blk, forward, 0)

    group = 8

    def blur_yz(it, g):
        v = g // (SUB // group)
        rows = pl.ds(pl.multiple_of(g * (group * y_chunk), 8), group * y_chunk)
        blocks = [yz[it, h, ch, rows, :] for h in range(2) for ch in range(CHUNKS)]
        value = jnp.concatenate(
            [block[r * y_chunk : (r + 1) * y_chunk] for r in range(group) for block in blocks], axis=0
        )
        value = from_right(value, wzc[v])
        return from_left(wyc[v], to_lanes(value, y_cells))

    def back_yz(it, g, blur):
        v = g // (SUB // group)
        rows = pl.ds(pl.multiple_of(g * (group * y_cells), 8), group * y_cells)
        ratios = to_lanes(meas[rows, :], y_cells) / blur
        value = to_rows(from_left(wytc[v], ratios), z_cells)
        value = from_right(value, wztc[v])
        rows = pl.ds(pl.multiple_of(g * (group * y_half), 8), group * y_half)
        for h in range(2):
            back_full[it, h, rows, :] = jnp.concatenate(
                [value[r : r + y_half] for r in range(h * y_half, value.shape[0], y_cells)], axis=0
            )

    def back_copy(it, v):
        rows = slice(v * SUB * y_half, (v + 1) * SUB * y_half)
        return remote(
            back_full.at[it, other, rows, :], back_recv.at[it, rows, :],
            b_send.at[it, v], b_recv.at[it, v], partner,
        )

    def back_x(it, ch):
        parts = []
        for y in range(y_chunk):
            rows = pl.ds(ch * y_chunk + y, 2 * SUB, stride=y_half)
            parts.append(
                jnp.concatenate([back_full[it, a, rows, :], back_recv[it, rows, :]], axis=0)
            )
        corr[it, :, ch * lanes : (ch + 1) * lanes] = from_left(mxtc[...], jnp.concatenate(parts, axis=1))
        for i, copy in enumerate(corr_copies(it, ch)[:4]):
            send_along(corr_plan[i][0], copy)

    def updated(it, ch):
        for i, copy in enumerate(corr_copies(it, ch)[2:]):
            take_along(corr_plan[2 + i][0], copy)
        cols = slice(ch * lanes, (ch + 1) * lanes)
        total = corr[it, EDGE : EDGE + SUB, cols] + jnp.concatenate([
            came[it, 4, :, cols] + came[it, 3, :, cols],
            came[it, 2, :, cols] + came[it, 5, :, cols],
        ], axis=0)
        return win[it, EDGE : EDGE + SUB, cols] * (total / VIEWS)

    def out_cols(ch, core):
        return pl.ds(pl.multiple_of(core * y_half + ch * y_chunk, 8), y_chunk)

    def out_copies(ch):
        src = out_half.at[:, ch * y_chunk : (ch + 1) * y_chunk, :]
        dst = out_ref.at[rows_here, out_cols(ch, a), :]
        own = pltpu.make_async_copy(src, dst, o_recv.at[ch, a, 0])
        mates = [
            remote(src, dst, o_send.at[ch, i], o_recv.at[ch, a, min(i, 1)], (to_x, 2 * c + par))
            for i, to_x in enumerate((x, lax.rem(x + 1, 4), lax.rem(x + 3, 4)))
        ]
        return own, mates

    flip = lax.rem(c, 2)
    odd = lax.rem(x + 1 - flip, 2)
    ahead = lax.rem(x - snake(2 * a + odd, c) + 4, 4)
    onward = lax.rem(x + 2 - ahead + 4, 4)
    onward_rows = pl.ds(odd * SUB + 8 * (ahead // 2), 8)
    odd_rows = pl.ds(odd * SUB, SUB)

    def onward_copies(ch):
        copies = []
        for h in range(2):
            part = out_ref.at[onward_rows, out_cols(ch, h), :]
            copies.append(remote(part, part, f_send.at[ch, h], o_recv.at[ch, h, 0], (onward, b)))
        return copies

    def send_on(ch):
        for h, copy in enumerate(onward_copies(ch)):
            await_bytes(out_ref.at[odd_rows, out_cols(ch, h), :], o_recv.at[ch, h, 1])
            copy.start()

    for it in range(ITERS):
        for ch in range(CHUNKS):
            x_copy(it, ch).wait_recv()
        if it == 0:
            def first(g, carry):
                blurred[g] = blur_yz(0, g)
                return carry

            lax.fori_loop(0, 2 * SUB // group, first, 0, unroll=2)
            await_bytes(meas, p2_recv)
        per_view = SUB // group
        for v in range(2):
            def both(g, carry):
                back_yz(it, g, blurred[g] if it == 0 else blur_yz(it, g))
                return carry

            lax.fori_loop(v * per_view, (v + 1) * per_view, both, 0, unroll=True)
            back_copy(it, v).start()
        for v in range(2):
            back_copy(it, v).wait_recv()
        for ch in range(CHUNKS):
            back_x(it, ch)
        def finish(ch):
            new = updated(it, ch)
            if it + 1 < ITERS:
                win[it + 1, EDGE : EDGE + SUB, ch * lanes : (ch + 1) * lanes] = new
                for i, copy in enumerate(halo_copies(it + 1, ch)[:4]):
                    send_along(halo_plan[i][0], copy)
                return
            for y in range(y_chunk):
                out_flat[ch, pl.ds(y, SUB, stride=y_chunk), :] = new[
                    :, y * z_cells : (y + 1) * z_cells
                ]
            out_half[:, ch * y_chunk : (ch + 1) * y_chunk, :] = out_flat[ch].reshape(
                SUB, y_chunk, z_cells
            )
            own, mates = out_copies(ch)
            for mate in mates[1:]:
                mate.start()

            @pl.when(a == par)
            def _():
                own.start()

            @pl.when(a != par)
            def _():
                mates[0].start()

        def move_on(ch):
            if it + 1 < ITERS:
                pass_on(it + 1, ch)
            else:
                send_on(ch)

        for t in range(CHUNKS + 3):
            if t < CHUNKS:
                merge(it, t)
            if 0 <= t - 1 < CHUNKS:
                finish(t - 1)
            if 0 <= t - 2 < CHUNKS:
                move_on(t - 2)
            if 0 <= t - 3 < CHUNKS and it + 1 < ITERS:
                blur_x(it + 1, t - 3)

    await_bytes(id_row.at[: row_size - 1], id1_send)
    await_bytes(id_all.at[: n_rows - 1], id2_send)
    await_bytes(exch.at[: n_blk - 1], p1_send)
    await_bytes(chosen.at[: n_blk - 1], p2_send)

    @pl.when(jnp.logical_not((a == x // 2) & (lax.rem(q, 2) == half)))
    def _():
        await_bytes(chosen.at[0], p2_send)

    @pl.when(a == par)
    def _():
        remote(est_part(other), est_half, est_send, est_recv, partner).wait_send()

    for copy in prm_copies:
        copy.wait_send()
    for it in range(ITERS):
        for ch in range(CHUNKS):
            for i in range(6):
                sent_along(halo_plan[i][0], halo_copies(it, ch)[i])
                sent_along(corr_plan[i][0], corr_copies(it, ch)[i])
            x_copy(it, ch).wait_send()
        for v in range(2):
            back_copy(it, v).wait_send()
    for ch in range(CHUNKS):
        own, mates = out_copies(ch)
        for copy in mates[1:] + onward_copies(ch):
            copy.wait_send()

        @pl.when(a != par)
        def _():
            mates[0].wait_send()

        for h in range(2):
            await_bytes(out_half.at[:, :y_chunk, :], o_recv.at[ch, h, 0])


def per_device(estimate, view_data, slot_block, offsets, taps):
    n_blk = lax.axis_size("blk")
    block_rows, y_cells, z_cells = estimate.shape
    row_size = 16 if n_blk % 16 == 0 else n_blk // 2
    n_rows = n_blk // row_size
    padded = max(row_size, 8)
    piece_rows = block_rows * y_cells // n_blk
    pieces = view_data.reshape(n_blk, piece_rows, z_cells)
    y_half = y_cells // 2
    y_chunk = y_half // CHUNKS
    width = y_half * z_cells
    vmem = pltpu.VMEM
    dma = pltpu.SemaphoreType.DMA
    regular = pltpu.SemaphoreType.REGULAR
    return pl.pallas_call(
        functools.partial(kernel, n_blk, row_size, y_cells, z_cells),
        out_shape=jax.ShapeDtypeStruct(estimate.shape, F32),
        in_specs=[
            pl.BlockSpec(memory_space=pltpu.SMEM),
            pl.BlockSpec(memory_space=pltpu.SMEM),
            pl.BlockSpec(memory_space=pltpu.VMEM),
            pl.BlockSpec(memory_space=pl.ANY),
            pl.BlockSpec(memory_space=pl.ANY),
        ],
        out_specs=pl.BlockSpec(memory_space=pl.ANY),
        scratch_shapes=[
            vmem((8, 128), jnp.int32),
            vmem((row_size, 8, 128), jnp.int32),
            vmem((n_rows, padded, 128), jnp.int32),
            vmem((8, 128), jnp.int32),
            pltpu.SMEM((8, 128), jnp.int32),
            vmem((n_blk, piece_rows, z_cells), F32),
            vmem((n_blk, piece_rows, z_cells), F32),
            vmem((2 * SUB * y_cells, z_cells), F32),
            vmem((8, 128), F32),
            vmem((2, VIEWS, 8, 128), F32),
            vmem((4 * SUB, 3 * WIN), BF16),
            vmem((WIN, 3 * 4 * SUB), BF16),
            vmem((2, y_cells, 3 * y_cells), BF16),
            vmem((2, y_cells, 3 * y_cells), BF16),
            vmem((2, 2 * z_cells, 2 * z_cells), BF16),
            vmem((2, 2 * z_cells, 2 * z_cells), BF16),
            vmem((SUB, y_half, z_cells), F32),
            vmem((SUB * y_half, z_cells), F32),
            vmem((ITERS, WIN, width), F32),
            vmem((ITERS, 2, CHUNKS, 2 * SUB * y_chunk, z_cells), F32),
            vmem((ITERS, CHUNKS, 2 * SUB * y_chunk, z_cells), F32),
            vmem((2 * SUB // 8, y_cells, 8 * z_cells), F32),
            vmem((ITERS, 2, 2 * SUB * y_half, z_cells), F32),
            vmem((ITERS, 2 * SUB * y_half, z_cells), F32),
            vmem((ITERS, WIN, width), F32),
            vmem((ITERS, 6, 8, width), F32),
            vmem((ITERS, 2, 8, width), F32),
            vmem((CHUNKS, SUB * y_chunk, z_cells), F32),
            vmem((SUB, y_half, z_cells), F32),
            dma, dma, dma, dma, dma,
            dma, dma, dma, dma,
            dma((7,)), dma((7,)), dma, dma,
            dma((ITERS, CHUNKS, 6)), dma((ITERS, CHUNKS, 6)),
            dma((ITERS, CHUNKS)), dma((ITERS, CHUNKS)),
            dma((ITERS, 2)), dma((ITERS, 2)),
            dma((ITERS, CHUNKS, 6)), dma((ITERS, CHUNKS, 6)),
            dma((CHUNKS, 3)), dma((CHUNKS, 2)), dma((CHUNKS, 2, 2)),
            regular, regular,
        ],
        compiler_params=pltpu.CompilerParams(
            collective_id=0, has_side_effects=True, vmem_limit_bytes=52 * 1024 * 1024
        ),
    )(slot_block, offsets, taps, estimate, pieces)


def solution(mesh):
    return jax.shard_map(
        per_device,
        mesh=mesh,
        in_specs=(
            P("blk", None, None),
            P("view", "blk", None, None),
            P("view", "blk"),
            P("view", "blk"),
            P("view", None, None),
        ),
        out_specs=P("blk", None, None),
        check_vma=False,
    )
```
